32 devices in a mesh: rep: 4 (over y, x), shard: 8 (over z, core).
Axes of the slice: x: 2, y: 2, z: 4, core: 2. Of those that a mesh axis runs over, the one named last changes fastest.
Arguments:
- hidden_in: bfloat16 [8192, 2048], P(('rep', 'shard')), may hold values from -6 to 6
- layer_vectors: bfloat16 [8192, 256], P(('rep', 'shard')), may hold values from -6 to 6
- positions: int32 [8192], P(('rep', 'shard')), may hold values from 0 to 2047, as said below
- cotangent: bfloat16 [8192, 2048], P(('rep', 'shard')), may hold values from -6 to 6
- model_gains: float32 [6, 2048], replicated, may hold values from 0.1 to 1.9
- head_gains: float32 [2, 256], replicated, may hold values from 0.1 to 1.9
- qkv_weight: bfloat16 [2048, 3072], P('shard'), may hold values from -0.125 to 0.125
- out_weight: bfloat16 [2048, 2048], P('shard'), may hold values from -0.125 to 0.125
- laurel_down: bfloat16 [2048, 64], P('shard'), may hold values from -0.125 to 0.125
- laurel_up: bfloat16 [2048, 64], P('shard'), may hold values from -0.75 to 0.75
- gate_up_weight: bfloat16 [2048, 16384], P('shard'), may hold values from -0.125 to 0.125
- down_weight: bfloat16 [2048, 8192], P('shard'), may hold values from -0.0625 to 0.0625
- layer_gate: bfloat16 [2048, 256], P('shard'), may hold values from -0.125 to 0.125
- layer_project: bfloat16 [2048, 256], P('shard'), may hold values from -0.375 to 0.375
Outputs:
- layer_out: bfloat16 [8192, 2048], P(('rep', 'shard'))
- grad_hidden: float32 [8192, 2048], P(('rep', 'shard'))
- grad_vectors: float32 [8192, 256], P(('rep', 'shard'))
- grad_model_gains: float32 [6, 2048], replicated
- grad_head_gains: float32 [2, 256], replicated
- grad_qkv: float32 [2048, 3072], P('shard')
- grad_out: float32 [2048, 2048], P('shard')
- grad_laurel_down: float32 [2048, 64], P('shard')
- grad_laurel_up: float32 [2048, 64], P('shard')
- grad_gate_up: float32 [2048, 16384], P('shard')
- grad_down: float32 [2048, 8192], P('shard')
- grad_layer_gate: float32 [2048, 256], P('shard')
- grad_layer_project: float32 [2048, 256], P('shard')
The draws below stay inside these ranges and needn't reach their ends.
Inputs may be any that keep to these rules, and one draw needn't show every extreme that they name: positions count the tokens before each token in its own document: 0 at a document's first token, one more at each following one; every sequence of 2048 tokens begins with a document, and one sequence is a single document of 2048 tokens.
All inputs are finite; a program needn't handle non-finite values.
Results may differ from the reference program's by a relative error of at most 0.024.
Values may be sent and summed in bfloat16 or wider, within the bound.
No kernel may reach another device: no remote copies, remote signals or barrier semaphores. Data moves between devices by JAX's collectives and lax.ppermute only.
A program may use at most 768 MiB of HBM per device.

```python
import math
import jax
import jax.numpy as jnp
from jax import lax

D = 2048
H = 8
KV = 2
HD = 256
FF = 8192
RANK = 64
PLE = 256
WINDOW = 512
SEQ = 2048
TOKENS = 8192
N_REP = 4


def draw_positions(key, part):
    first_key, second_key = jax.random.split(jax.random.fold_in(key, 11))
    third_key = jax.random.fold_in(key, 23)
    powers = jax.random.randint(first_key, (TOKENS,), 1, 11)
    limits = jnp.left_shift(jnp.ones((TOKENS,), jnp.int32), powers)
    lengths = jax.random.randint(second_key, (TOKENS,), 0, 1048576) % limits + 1
    doc_starts = jnp.cumsum(lengths) - lengths
    token_index = jnp.arange(TOKENS, dtype=jnp.int32)
    start_marks = jnp.zeros((TOKENS,), jnp.int32).at[doc_starts].set(1, mode='drop')
    chosen = jax.random.randint(third_key, (), 0, TOKENS // SEQ)
    start_marks = jnp.where(token_index // SEQ == chosen, 0, start_marks)
    start_marks = jnp.where(token_index % SEQ == 0, 1, start_marks)
    doc_begin = lax.cummax(jnp.where(start_marks == 1, token_index, 0), axis=0)
    return (token_index - doc_begin).astype(jnp.int32)


def block_levels(own_key, shape, cuts, smallest, top_value):
    loudness, own = 1.0, jax.random.fold_in(own_key, 6)
    for dim, shards_of in cuts:
        draws = jnp.exp(jax.random.uniform(jax.random.fold_in(own, dim), (shards_of,), jnp.float32, smallest / len(cuts), top_value / len(cuts)))
        loudness = loudness * jnp.repeat(draws, shape[dim] // shards_of).reshape([-1 if axis == dim else 1 for axis in range(len(shape))])
    return loudness


def bell_draw(stream_key, extent, scale, reach, cuts=(), held_as=jnp.bfloat16):
    values = jax.random.normal(stream_key, extent, jnp.float32) * scale
    if len(cuts) > 0:
        values = block_levels(stream_key, extent, cuts, -0.22, 0.18) * values
    return jnp.clip(values, min=-reach, max=reach).astype(held_as)


def setup_inputs(seed: int = 0) -> dict:
    arg_keys = jax.random.split(jax.random.key(seed), 15)
    hidden_in = bell_draw(arg_keys[0], (TOKENS, D), 1.0, 6.0, ((0, 32),))
    layer_vectors = bell_draw(arg_keys[1], (TOKENS, PLE), 1.0, 6.0, ((0, 32),))
    positions = draw_positions(jax.random.fold_in(arg_keys[14], 71), 0)
    cotangent = bell_draw(arg_keys[3], (TOKENS, D), 1.0, 6.0, ((0, 32),))
    model_gains = jnp.clip(1.0 + 0.18 * jax.random.normal(arg_keys[4], (6, D), jnp.float32), 0.1, 1.9)
    head_gains = jnp.clip(1.0 + 0.18 * jax.random.normal(arg_keys[5], (2, HD), jnp.float32), 0.1, 1.9)
    qkv_weight = bell_draw(arg_keys[6], (D, (H + 2 * KV) * HD), D ** -0.5, 0.125, ((0, 8),))
    out_weight = bell_draw(arg_keys[7], (D, H * HD), (H * HD) ** -0.5, 0.125, ((0, 8),))
    laurel_down = bell_draw(arg_keys[8], (D, RANK), D ** -0.5, 0.125, ((0, 8),))
    laurel_up = bell_draw(arg_keys[9], (D, RANK), RANK ** -0.5, 0.75, ((0, 8),))
    gate_up_weight = bell_draw(arg_keys[10], (D, 2 * FF), D ** -0.5, 0.125, ((0, 8),))
    down_weight = bell_draw(arg_keys[11], (D, FF), FF ** -0.5, 0.0625, ((0, 8),))
    layer_gate = bell_draw(arg_keys[12], (D, PLE), D ** -0.5, 0.125, ((0, 8),))
    layer_project = bell_draw(arg_keys[13], (D, PLE), PLE ** -0.5, 0.375, ((0, 8),))
    return dict(hidden_in=hidden_in, layer_vectors=layer_vectors, positions=positions, cotangent=cotangent, model_gains=model_gains, head_gains=head_gains, qkv_weight=qkv_weight, out_weight=out_weight, laurel_down=laurel_down, laurel_up=laurel_up, gate_up_weight=gate_up_weight, down_weight=down_weight, layer_gate=layer_gate, layer_project=layer_project)


@jax.custom_vjp
def low(v):
    return lax.optimization_barrier(v.astype(jnp.bfloat16)).astype(jnp.float32)

@jax.custom_vjp
def low_back(v):
    return v

def low_keep(v):
    return (low(v), None)

def low_pass(kept, grad):
    return (grad,)

def back_keep(v):
    return (v, None)

def back_low(kept, grad):
    return (low(grad),)
low.defvjp(low_keep, low_pass)
low_back.defvjp(back_keep, back_low)
EPSILON = 1e-06
HIGHEST = lax.Precision.HIGHEST
SQRT_HALF = 0.7071067811865476

def scaled_norm(values, gain_row):
    return values * lax.rsqrt(lax.optimization_barrier(jnp.mean(values * values, axis=-1, keepdims=True)) + EPSILON) * gain_row

def rotate(values, cosine, sine_part):
    half_dim = values.shape[-1] // 2
    first_half = values[..., :half_dim]
    second_half = values[..., half_dim:]
    return jnp.concatenate([first_half * cosine - second_half * sine_part, second_half * cosine + first_half * sine_part], axis=-1)

def rope_tables(positions, head_dim):
    half_dim = head_dim // 2
    frequency = jnp.exp(jnp.arange(half_dim, dtype=jnp.float32) * (-2.0 * math.log(10000.0) / head_dim))
    phase_angle = positions.astype(jnp.float32)[:, None] * frequency[None, :]
    return (jnp.cos(phase_angle)[:, None, :], jnp.sin(phase_angle)[:, None, :])

def product(left_side, right_side):
    return jnp.dot(left_side, right_side, precision=HIGHEST)

def product_nt(left_side, right_side):
    return lax.dot_general(left_side, right_side, (((1,), (1,)), ((), ())), precision=HIGHEST)

def attend(queries, key_heads, value_heads, places):
    block_rows = math.gcd(SEQ, 512)
    group_size = H // KV
    score_scale = 1.0 / math.sqrt(HD)
    keys_pad = jnp.pad(key_heads, ((WINDOW, 0), (0, 0), (0, 0)))
    values_pad = jnp.pad(value_heads, ((WINDOW, 0), (0, 0), (0, 0)))
    offsets = jnp.arange(block_rows, dtype=jnp.int32)[:, None] + WINDOW - jnp.arange(block_rows + WINDOW, dtype=jnp.int32)[None, :]

    def one_block(block_index):
        row_start = (block_index * block_rows).astype(jnp.int32)
        query_block = lax.dynamic_slice_in_dim(queries, row_start, block_rows, 0).reshape(block_rows, KV, group_size, HD)
        key_block = lax.dynamic_slice_in_dim(keys_pad, row_start, block_rows + WINDOW, 0)
        value_block = lax.dynamic_slice_in_dim(values_pad, row_start, block_rows + WINDOW, 0)
        place_block = lax.dynamic_slice_in_dim(places, row_start, block_rows, 0)
        valid_keys = (offsets >= 0) & (offsets < WINDOW) & (offsets <= place_block[:, None])
        scores = low_back(jnp.einsum('qcgd,kcd->cgqk', query_block, key_block, precision=HIGHEST) * score_scale)
        masked = jnp.where(valid_keys, scores, -1e+30)
        row_max = lax.optimization_barrier(jnp.max(masked, axis=-1, keepdims=True))
        exponents = jnp.exp(masked - row_max)
        probabilities = exponents / lax.optimization_barrier(jnp.sum(exponents, axis=-1, keepdims=True))
        mixed = jnp.einsum('cgqk,kcd->qcgd', low(probabilities), value_block, precision=HIGHEST)
        return mixed.reshape(block_rows, H * HD)
    blocks = lax.map(jax.checkpoint(one_block), jnp.arange(SEQ // block_rows, dtype=jnp.int32))
    return blocks.reshape(SEQ, H * HD)

def layer(token_in, extra_in, places, model_gains, head_gains, qkv_weight, out_weight, laurel_down, laurel_up, gate_up_weight, down_weight, layer_gate, layer_project):
    first_norm = low(scaled_norm(token_in, model_gains[0]))
    proj_qkv = low_back(product(first_norm, qkv_weight))
    query_pre = proj_qkv[:, :H * HD].reshape(SEQ, H, HD)
    key_pre = proj_qkv[:, H * HD:(H + KV) * HD].reshape(SEQ, KV, HD)
    value_pre = proj_qkv[:, (H + KV) * HD:].reshape(SEQ, KV, HD)
    cosine, sine_part = rope_tables(places, HD)
    queries = low(rotate(scaled_norm(query_pre, head_gains[0]), cosine, sine_part))
    key_heads = low(rotate(scaled_norm(key_pre, head_gains[1]), cosine, sine_part))
    value_heads = low(value_pre)
    mixed = low(low_back(attend(queries, key_heads, value_heads, places)))
    attn_out = scaled_norm(low_back(product_nt(mixed, out_weight)), model_gains[1])
    middle = low(low_back(product(first_norm, laurel_down)))
    side_out = scaled_norm(low_back(product_nt(middle, laurel_up)), model_gains[2])
    first_sum = (token_in + attn_out + first_norm + side_out) * SQRT_HALF
    second_norm = low(scaled_norm(first_sum, model_gains[3]))
    gate_up = low_back(product(second_norm, gate_up_weight))
    hidden = low(jax.nn.gelu(gate_up[:, :FF], approximate=True) * gate_up[:, FF:])
    second_sum = first_sum + scaled_norm(low_back(product_nt(hidden, down_weight)), model_gains[4])
    ple_pre = low_back(product(low(second_sum), layer_gate))
    gated = low(jax.nn.gelu(ple_pre, approximate=True) * extra_in)
    return second_sum + scaled_norm(low_back(product_nt(gated, layer_project)), model_gains[5])

def reference(hidden_in, layer_vectors, positions, cotangent, model_gains, head_gains, qkv_weight, out_weight, laurel_down, laurel_up, gate_up_weight, down_weight, layer_gate, layer_project):
    params = tuple((element.astype(jnp.float32) for element in (model_gains, head_gains, qkv_weight, out_weight, laurel_down, laurel_up, gate_up_weight, down_weight, layer_gate, layer_project)))
    inputs = (hidden_in.astype(jnp.float32).reshape(N_REP, SEQ, D), layer_vectors.astype(jnp.float32).reshape(N_REP, SEQ, PLE), positions.reshape(N_REP, SEQ), cotangent.astype(jnp.float32).reshape(N_REP, SEQ, D))

    def one_sequence(totals, sequence_items):
        tokens, extras, places, upstream = sequence_items

        def forward(token_in, extra_in, *weights):
            return layer(token_in, extra_in, places, *weights)
        output, pullback = jax.vjp(forward, tokens, extras, *params)
        gradients = pullback(upstream)
        totals = tuple((running + fresh for running, fresh in zip(totals, gradients[2:])))
        return (totals, (output, gradients[0], gradients[1]))
    start_totals = tuple((jnp.zeros_like(element) for element in params))
    totals, (outputs, grad_hidden, grad_vectors) = lax.scan(one_sequence, start_totals, inputs)
    return (outputs.reshape(TOKENS, D).astype(jnp.bfloat16), grad_hidden.reshape(TOKENS, D), grad_vectors.reshape(TOKENS, PLE), totals[0], totals[1], totals[2], totals[3], totals[4], totals[5], totals[6], totals[7], totals[8], totals[9])
```

```python
import math

import jax
import jax.numpy as jnp
import numpy as np
from jax import lax
from jax.sharding import Mesh
from jax.sharding import PartitionSpec as P

WINDOW = 512
EPSILON = 1e-06
SQRT_HALF = 0.7071067811865476
BF = jnp.bfloat16
F32 = jnp.float32
REP = ("ra", "rb")


def scaled_norm(values, gain_row):
    return (
        values * lax.rsqrt(jnp.mean(values * values, axis=-1, keepdims=True) + EPSILON) * gain_row
    )


def rotate(values, cosine, sine_part):
    half_dim = values.shape[-1] // 2
    first_half = values[..., :half_dim]
    second_half = values[..., half_dim:]
    return jnp.concatenate(
        [
            first_half * cosine - second_half * sine_part,
            second_half * cosine + first_half * sine_part,
        ],
        axis=-1,
    )


def rope_tables(positions, head_dim):
    half_dim = head_dim // 2
    frequency = jnp.exp(
        jnp.arange(half_dim, dtype=jnp.float32) * (-2.0 * math.log(10000.0) / head_dim)
    )
    phase_angle = positions.astype(jnp.float32)[:, None] * frequency[None, :]
    return (jnp.cos(phase_angle)[:, None, :], jnp.sin(phase_angle)[:, None, :])


def dot_plain(left_side, right_side):
    return jnp.dot(left_side, right_side, preferred_element_type=jnp.float32)


def dot_right_t(left_side, right_side):
    return lax.dot_general(
        left_side, right_side, (((1,), (1,)), ((), ())), preferred_element_type=jnp.float32
    )


def dot_left_t(left_side, right_side):
    return lax.dot_general(
        left_side, right_side, (((0,), (0,)), ((), ())), preferred_element_type=jnp.float32
    )


def gelu_tanh(values):
    return jax.nn.gelu(values, approximate=True)


def after(value, *others):
    return lax.optimization_barrier((value,) + others)[0]


def swap(value, axis):
    return lax.ppermute(value, axis, [(0, 1), (1, 0)])


def square():
    return lax.axis_size("ra") == 2 and lax.axis_size("rb") == 2


def rep_count():
    return lax.axis_size("ra") * lax.axis_size("rb")


def rep_id():
    return lax.axis_index("ra") * lax.axis_size("rb") + lax.axis_index("rb")


def rep_of(k):
    return rep_id() ^ k if square() else k


def rep_gather(value):
    if not square():
        whole = lax.all_gather(value, REP, axis=0)
        return [whole[k] for k in range(rep_count())]
    half = value.shape[0] // 2
    from_b = swap(value, "rb")
    from_a = swap(value, "ra")
    far_one = swap(from_a[:half], "rb")
    far_two = swap(from_b[half:], "ra")
    return [value, from_b, from_a, jnp.concatenate([far_one, far_two], axis=0)]


def rep_scatter(parts):
    if not square():
        return lax.psum_scatter(jnp.stack(parts), REP, scatter_dimension=0).astype(F32)
    half = parts[3].shape[0] // 2
    far_one = swap(parts[3][:half], "rb")
    far_two = swap(parts[3][half:], "ra")
    to_b = jnp.concatenate(
        [parts[1][:half].astype(F32), parts[1][half:].astype(F32) + far_two.astype(F32)], axis=0
    ).astype(BF)
    to_a = jnp.concatenate(
        [parts[2][:half].astype(F32) + far_one.astype(F32), parts[2][half:].astype(F32)], axis=0
    ).astype(BF)
    from_b = swap(to_b, "rb")
    from_a = swap(to_a, "ra")
    return parts[0].astype(F32) + from_b.astype(F32) + from_a.astype(F32)


def shift(value, steps):
    count = lax.axis_size("line")
    return lax.ppermute(value, "line", [(i, (i + steps) % count) for i in range(count)])


def line_slots(value):
    count = lax.axis_size("line")
    place = lax.axis_index("line")
    ups, downs = [value], [value]
    for s in range(1, count):
        ups.append(lax.ppermute(ups[-1], "line", [(i, i + 1) for i in range(s - 1, count - 1)]))
        downs.append(lax.ppermute(downs[-1], "line", [(i + 1, i) for i in range(0, count - s)]))
    first = (ups[1], downs[1])
    return [value] + [
        jnp.where(place >= s, ups[s], downs[count - s]) for s in range(1, count)
    ], first


def place_slots(slots):
    count = lax.axis_size("line")
    place = lax.axis_index("line")
    whole = jnp.zeros((count,) + slots[0].shape, slots[0].dtype)
    for s in range(count):
        whole = lax.dynamic_update_index_in_dim(whole, slots[s], (place - s) % count, 0)
    return whole.reshape((count * slots[0].shape[0],) + slots[0].shape[1:])


def line_scatter(blocks):
    count = lax.axis_size("line")
    place = lax.axis_index("line")

    def block(j):
        return lax.dynamic_index_in_dim(blocks, jnp.clip(j, 0, count - 1), 0, keepdims=False)

    going_up = going_down = None
    for t in range(1, count):
        up = block(place + count - t)
        down = block(place - count + t)
        if going_up is not None:
            up = (up.astype(F32) + going_up.astype(F32)).astype(BF)
            down = (down.astype(F32) + going_down.astype(F32)).astype(BF)
        going_up = lax.ppermute(up, "line", [(i, i + 1) for i in range(t)])
        going_down = lax.ppermute(down, "line", [(count - 1 - i, count - 2 - i) for i in range(t)])
    own = block(place).astype(F32)
    return (own + going_up.astype(F32) + going_down.astype(F32)).astype(BF)


def sum_everywhere(value):
    sizes = [lax.axis_size(a) for a in ("core", "rb", "ra", "line")]
    if any(n & (n - 1) for n in sizes):
        return lax.psum(value, ("ra", "rb", "line", "core"))
    for axis, n in zip(("core", "rb", "ra", "line"), sizes):
        step = 1
        while step < n:
            value = value + lax.ppermute(value, axis, [(i, i ^ step) for i in range(n)])
            step *= 2
    return value


def by_core(mine, other, axis):
    first = lax.axis_index("core") == 0
    return jnp.concatenate(
        [jnp.where(first, mine, other), jnp.where(first, other, mine)], axis=axis
    )


def pick(pair, which):
    return jnp.where(which == 0, pair[0], pair[1])


def body(
    hidden_in,
    layer_vectors,
    positions,
    cotangent,
    model_gains,
    head_gains,
    qkv_weight,
    out_weight,
    laurel_down,
    laurel_up,
    gate_up_weight,
    down_weight,
    layer_gate,
    layer_project,
):
    tokens, width = hidden_in.shape
    head_dim = head_gains.shape[1]
    query_heads = out_weight.shape[1] // head_dim
    kv_heads = (qkv_weight.shape[1] // head_dim - query_heads) // 2
    group = query_heads // kv_heads
    ffn_units = down_weight.shape[1]
    rank = laurel_down.shape[1]
    ple = layer_gate.shape[1]
    score_scale = 1.0 / math.sqrt(head_dim)
    reps = rep_count()
    line = lax.axis_size("line")
    cores = 2
    core = lax.axis_index("core")
    rep = rep_id()
    place = lax.axis_index("line")
    weight_rows = qkv_weight.shape[0]
    sub = weight_rows // reps
    group_width = group * head_dim
    part_width = group_width + 2 * head_dim
    small_width = rank + ple
    units = ffn_units // (reps * cores)
    pair = 2 * tokens
    assert kv_heads == cores and pair >= WINDOW

    qkv_rows = lax.dynamic_slice_in_dim(qkv_weight, rep * sub, sub, 0)
    out_rows = lax.dynamic_slice_in_dim(out_weight, rep * sub, sub, 0)

    def qkv_columns(rows, c):
        return jnp.concatenate(
            [
                lax.dynamic_slice_in_dim(rows, c * group_width, group_width, 1),
                lax.dynamic_slice_in_dim(
                    rows, query_heads * head_dim + c * head_dim, head_dim, 1
                ),
                lax.dynamic_slice_in_dim(
                    rows, (query_heads + kv_heads) * head_dim + c * head_dim, head_dim, 1
                ),
            ],
            axis=1,
        )

    down_small = jnp.concatenate([laurel_down, layer_gate], axis=1)
    up_small = jnp.concatenate([laurel_up, layer_project], axis=1)
    small_pair = (
        lax.dynamic_slice_in_dim(down_small, rep * sub, sub, 0),
        lax.dynamic_slice_in_dim(up_small, rep * sub, sub, 0),
    )

    def out_columns(rows, c):
        return jnp.concatenate(
            [
                lax.dynamic_slice_in_dim(rows, c * group_width, group_width, 1),
                pick(small_pair, c),
            ],
            axis=1,
        )

    def both_cores_rows(columns, rows):
        mine = columns(rows, core)
        other = swap(columns(rows, 1 - core), "core")
        first = core == 0
        return jnp.stack([jnp.where(first, mine, other), jnp.where(first, other, mine)])

    def spread(block, line_after=None, rep_after=None):
        if line_after is not None:
            block = after(block, *line_after)
        slots = [block] + [shift(block, s) for s in range(1, line)]
        on_line = slots[1:]
        whole = jnp.zeros((line, cores, reps, sub, block.shape[-1]), BF)
        last = None
        for s in range(line):
            slot = slots[s] if rep_after is None else after(slots[s], *rep_after)
            pieces = rep_gather(slot)
            last = pieces[1:]
            for k in range(reps):
                whole = lax.dynamic_update_slice(
                    whole,
                    pieces[k][None, :, None],
                    ((place - s) % line, 0, rep_of(k), 0, 0),
                )
        return whole.reshape(line * cores * reps * sub, block.shape[-1]), on_line, last

    qkv_block = both_cores_rows(qkv_columns, qkv_rows)
    out_block = both_cores_rows(out_columns, out_rows)
    qkv_part, qkv_line, qkv_last = spread(qkv_block)
    out_small, out_line, out_last = spread(out_block, qkv_line, qkv_last)
    out_part = out_small[:, :group_width]
    small_mine = out_small[:, group_width:]
    small_other = swap(small_mine, "core")
    first_core = core == 0
    down_small_full = jnp.where(first_core, small_mine, small_other)
    up_small_full = jnp.where(first_core, small_other, small_mine)
    down_low_full, gate_layer_full = down_small_full[:, :rank], down_small_full[:, rank:]
    up_low_full, project_full = up_small_full[:, :rank], up_small_full[:, rank:]

    def ffn_columns(c):
        start = (rep * cores + c) * units
        return [
            lax.dynamic_slice_in_dim(gate_up_weight, start, units, 1),
            lax.dynamic_slice_in_dim(gate_up_weight, ffn_units + start, units, 1),
            lax.dynamic_slice_in_dim(down_weight, start, units, 1),
        ]

    ffn_mine = ffn_columns(core)
    ffn_sent = ffn_columns(1 - core)
    ffn_whole = []
    previous = out_line
    for mine, sent in zip(ffn_mine, ffn_sent):
        block = by_core(mine, swap(sent, "core"), 0)
        slots, previous = line_slots(after(block, *previous))
        ffn_whole.append(place_slots(slots))
    gate_weight, up_weight, down_cols = ffn_whole
    gate_up_cols = jnp.concatenate([gate_weight, up_weight], axis=1)

    hidden_pair = jnp.concatenate([hidden_in, swap(hidden_in, "core")], axis=0)
    pos_pair = jnp.concatenate([positions, swap(positions, "core")], axis=0)
    steps = jnp.arange(tokens, dtype=jnp.int32)
    index = jnp.concatenate([core * tokens + steps, (1 - core) * tokens + steps])
    hidden_f = hidden_in.astype(F32)
    first_pair = scaled_norm(hidden_pair.astype(F32), model_gains[0]).astype(BF)
    normed_one, norm_one_pull = jax.vjp(scaled_norm, hidden_f, model_gains[0])
    first_norm = normed_one.astype(BF)
    proj = dot_plain(first_pair, qkv_part)
    query_pre = proj[:, :group_width].reshape(pair, group, head_dim)
    key_pre = proj[:, group_width : group_width + head_dim].reshape(pair, 1, head_dim)
    value_own = proj[:, group_width + head_dim :].astype(BF)
    cosine, sine_part = rope_tables(pos_pair, head_dim)

    def prepare(query_in, key_in, query_gain, key_gain):
        return (
            rotate(scaled_norm(query_in, query_gain), cosine, sine_part),
            rotate(scaled_norm(key_in, key_gain), cosine, sine_part),
        )

    (query_rot, key_rot), prepare_pull = jax.vjp(
        prepare, query_pre, key_pre, head_gains[0], head_gains[1]
    )
    query_low = query_rot.astype(BF)
    own_keys = jnp.concatenate([key_rot.astype(BF).reshape(pair, head_dim), value_own], axis=1)
    up_line = [(i, i + 1) for i in range(line - 1)]
    earlier = lax.ppermute(own_keys, "line", up_line)
    all_keys = jnp.concatenate([earlier, own_keys], axis=0)
    key_all = all_keys[:, :head_dim]
    value_all = all_keys[:, head_dim:]
    key_index = jnp.concatenate([index - pair, index])
    offsets = index[:, None] - key_index[None, :]
    valid_keys = (offsets >= 0) & (offsets < WINDOW) & (offsets <= pos_pair[:, None])

    def masked_scores():
        raw = jnp.einsum("qgd,kd->gqk", query_low, key_all, preferred_element_type=F32)
        return jnp.where(valid_keys, raw * score_scale, -1e30)

    scores = masked_scores()
    row_max = jnp.max(scores, axis=-1, keepdims=True)
    exponents = jnp.exp(scores - row_max)
    row_total = jnp.sum(exponents, axis=-1, keepdims=True)
    log_total = row_max + jnp.log(row_total)
    probs_low = (exponents / row_total).astype(BF)
    mixed = jnp.einsum("gqk,kd->qgd", probs_low, value_all, preferred_element_type=F32)
    mixed_low = mixed.reshape(pair, group_width).astype(BF)
    attn_sum = dot_right_t(mixed_low, out_part)
    attn_pre = attn_sum[:tokens] + swap(attn_sum[tokens:], "core")
    attn_out, attn_pull = jax.vjp(scaled_norm, attn_pre, model_gains[1])
    middle = dot_plain(first_norm, down_low_full).astype(BF)
    side_pre = dot_right_t(middle, up_low_full)
    side_out, side_pull = jax.vjp(scaled_norm, side_pre, model_gains[2])
    first_sum = (hidden_f + attn_out + first_norm.astype(F32) + side_out) * SQRT_HALF
    normed_two, norm_two_pull = jax.vjp(scaled_norm, first_sum, model_gains[3])

    def plane_gather(value):
        chunks = []
        for block in rep_gather(value):
            chunks += [block, swap(block, "core")]
        return jnp.concatenate(chunks, axis=0)

    def plane_scatter(whole):
        parts = []
        for k in range(reps):
            mine = whole[k * pair : k * pair + tokens]
            theirs = swap(whole[k * pair + tokens : (k + 1) * pair], "core")
            parts.append((mine.astype(F32) + theirs.astype(F32)).astype(BF))
        return rep_scatter(parts)

    second_all = plane_gather(normed_two.astype(BF))
    gate_up = dot_plain(second_all, gate_up_cols)

    def gated_units(gate_and_up):
        return gelu_tanh(gate_and_up[:, :units]) * gate_and_up[:, units:]

    hidden_val, hidden_pull = jax.vjp(gated_units, gate_up)
    hidden_low = hidden_val.astype(BF)
    ffn_pre = plane_scatter(dot_right_t(hidden_low, down_cols).astype(BF))
    ffn_out, ffn_pull = jax.vjp(scaled_norm, ffn_pre, model_gains[4])
    second_sum = first_sum + ffn_out
    second_low = second_sum.astype(BF)
    ple_pre = dot_plain(second_low, gate_layer_full)

    def gate_vectors(pre_values, vector_values):
        return gelu_tanh(pre_values) * vector_values

    gated_val, gated_pull = jax.vjp(gate_vectors, ple_pre, layer_vectors.astype(F32))
    gated_low = gated_val.astype(BF)
    last_pre = dot_right_t(gated_low, project_full)
    last_out, last_pull = jax.vjp(scaled_norm, last_pre, model_gains[5])
    layer_out = (second_sum + last_out).astype(BF)

    upstream = cotangent.astype(F32)
    d_last, grad_gain_five = last_pull(upstream)
    d_last_low = d_last.astype(BF)
    d_gated = dot_plain(d_last_low, project_full)
    d_ple_pre, grad_vectors = gated_pull(d_gated)
    d_ple_low = d_ple_pre.astype(BF)
    d_second = upstream + dot_right_t(d_ple_low, gate_layer_full)
    d_ffn, grad_gain_four = ffn_pull(d_second)
    d_ffn_all = plane_gather(d_ffn.astype(BF))
    d_hidden = dot_plain(d_ffn_all, down_cols)
    (d_gate_up,) = hidden_pull(d_hidden)
    d_gate_low = d_gate_up.astype(BF)

    def ffn_gradient(term):
        mine = line_scatter(term.reshape(line, cores * weight_rows, units))
        halves = mine.reshape(cores, weight_rows, units)
        keep = pick(halves, core)
        other = swap(pick(halves, 1 - core), "core")
        return by_core(keep, other, 1)

    def lay_out(blocks, total):
        out = jnp.zeros((weight_rows, total), F32)
        for block, start in blocks:
            out = lax.dynamic_update_slice(out, block.astype(F32), (0, start))
        return out

    def spread_columns(mine, offset):
        return [
            (block, offset + rep_of(k) * cores * units)
            for k, block in enumerate(rep_gather(mine))
        ]

    down_own = ffn_gradient(dot_left_t(d_ffn_all, hidden_low).astype(BF))
    d_second_norm = plane_scatter(dot_right_t(d_gate_low, gate_up_cols).astype(BF))
    gate_up_terms = dot_left_t(second_all, d_gate_low).astype(BF)
    gate_own = ffn_gradient(gate_up_terms[:, :units])
    up_own = ffn_gradient(gate_up_terms[:, units:])
    grad_down = lay_out(spread_columns(down_own, 0), ffn_units)
    grad_gate_up = lay_out(
        spread_columns(gate_own, 0) + spread_columns(up_own, ffn_units), 2 * ffn_units
    )

    d_first_part, grad_gain_three = norm_two_pull(d_second_norm)
    d_branch = (d_second + d_first_part) * SQRT_HALF
    d_side, grad_gain_two = side_pull(d_branch)
    d_side_low = d_side.astype(BF)
    d_middle_low = dot_plain(d_side_low, up_low_full).astype(BF)
    d_attn, grad_gain_one = attn_pull(d_branch)
    d_attn_low = d_attn.astype(BF)
    d_attn_pair = jnp.concatenate([d_attn_low, swap(d_attn_low, "core")], axis=0)
    d_mixed_low = dot_plain(d_attn_pair, out_part).astype(BF).reshape(pair, group, head_dim)
    probabilities = jnp.exp(masked_scores() - log_total)
    d_probs = jnp.einsum("qgd,kd->gqk", d_mixed_low, value_all, preferred_element_type=F32)
    d_values = jnp.einsum("gqk,qgd->kd", probs_low, d_mixed_low, preferred_element_type=F32)
    row_dot = jnp.sum(probabilities * d_probs, axis=-1, keepdims=True)
    d_scores = (probabilities * (d_probs - row_dot)).astype(BF)
    d_queries = (
        jnp.einsum("gqk,kd->qgd", d_scores, key_all, preferred_element_type=F32) * score_scale
    )
    d_keys = (
        jnp.einsum("gqk,qgd->kd", d_scores, query_low, preferred_element_type=F32) * score_scale
    )
    key_grads = jnp.concatenate([d_keys, d_values], axis=1)
    down_line = [(i + 1, i) for i in range(line - 1)]
    returned = lax.ppermute(key_grads[:pair].astype(BF), "line", down_line)
    own_grads = key_grads[pair:] + returned.astype(F32)
    d_query_pre, d_key_pre, grad_query_gain, grad_key_gain = prepare_pull(
        (d_queries, own_grads[:, :head_dim].reshape(pair, 1, head_dim))
    )
    d_proj = jnp.concatenate(
        [
            d_query_pre.reshape(pair, group_width),
            d_key_pre.reshape(pair, head_dim),
            own_grads[:, head_dim:],
        ],
        axis=1,
    ).astype(BF)
    norm_sum = dot_right_t(d_proj, qkv_part)
    d_first_norm = (
        norm_sum[:tokens]
        + swap(norm_sum[tokens:], "core")
        + dot_right_t(d_middle_low, down_low_full)
        + d_branch
    )
    d_input_part, grad_gain_zero = norm_one_pull(d_first_norm)
    grad_hidden = d_branch + d_input_part

    def reduce_rows(term):
        blocks = term.reshape(line, cores, reps, sub, term.shape[-1])
        parts = [
            lax.dynamic_index_in_dim(blocks, rep_of(k), 2, keepdims=False) for k in range(reps)
        ]
        mine = line_scatter(rep_scatter(parts).astype(BF))
        keep = pick(mine, core)
        other = swap(pick(mine, 1 - core), "core")
        first = core == 0
        both = jnp.stack([jnp.where(first, keep, other), jnp.where(first, other, keep)])
        whole = jnp.zeros((cores, reps, sub, term.shape[-1]), F32)
        for k, block in enumerate(rep_gather(jnp.swapaxes(both, 0, 1))):
            whole = lax.dynamic_update_slice(
                whole,
                jnp.swapaxes(block, 0, 1)[:, None].astype(F32),
                (0, rep_of(k), 0, 0),
            )
        return whole.reshape(cores, weight_rows, term.shape[-1])

    small_terms = (
        jnp.concatenate(
            [dot_left_t(first_norm, d_middle_low), dot_left_t(second_low, d_ple_low)], axis=1
        ).astype(BF),
        jnp.concatenate(
            [dot_left_t(d_side_low, middle), dot_left_t(d_last_low, gated_low)], axis=1
        ).astype(BF),
    )
    small_term = (
        pick(small_terms, core).astype(F32)
        + swap(pick(small_terms, 1 - core), "core").astype(F32)
    ).astype(BF)
    out_term = dot_left_t(d_attn_pair, mixed_low).astype(BF)
    out_red = reduce_rows(jnp.concatenate([out_term, small_term], axis=1))
    qkv_red = reduce_rows(dot_left_t(first_pair, d_proj).astype(BF))
    grad_qkv = jnp.concatenate(
        [qkv_red[c, :, :group_width] for c in range(cores)]
        + [qkv_red[c, :, group_width : group_width + head_dim] for c in range(cores)]
        + [qkv_red[c, :, group_width + head_dim :] for c in range(cores)],
        axis=1,
    )
    grad_out = jnp.concatenate([out_red[c, :, :group_width] for c in range(cores)], axis=1)
    grad_laurel_down = out_red[0, :, group_width : group_width + rank]
    grad_layer_gate = out_red[0, :, group_width + rank :]
    grad_laurel_up = out_red[1, :, group_width : group_width + rank]
    grad_layer_project = out_red[1, :, group_width + rank :]

    model_part = jnp.stack(
        [
            grad_gain_zero,
            grad_gain_one,
            grad_gain_two,
            grad_gain_three,
            grad_gain_four,
            grad_gain_five,
        ]
    )
    head_part = jnp.stack([grad_query_gain, grad_key_gain])
    gains = sum_everywhere(
        jnp.concatenate([model_part.reshape(-1, head_dim), head_part], axis=0)
    )
    grad_model_gains = gains[: -head_part.shape[0]].reshape(model_part.shape)
    grad_head_gains = gains[-head_part.shape[0] :]
    return (
        layer_out,
        grad_hidden,
        grad_vectors,
        grad_model_gains,
        grad_head_gains,
        grad_qkv,
        grad_out,
        grad_laurel_down,
        grad_laurel_up,
        grad_gate_up,
        grad_down,
        grad_layer_gate,
        grad_layer_project,
    )


def solution(mesh):
    reps, shards = mesh.shape["rep"], mesh.shape["shard"]
    fine = Mesh(
        np.asarray(mesh.devices).reshape(reps // 2, 2, shards // 2, 2), ("ra", "rb", "line", "core")
    )
    rows = P(("ra", "rb", "line", "core"), None)
    owned = P(("line", "core"), None)
    return jax.shard_map(
        body,
        mesh=fine,
        in_specs=(rows, rows, P(("ra", "rb", "line", "core")), rows, P(), P()) + (owned,) * 8,
        out_specs=(rows, rows, rows, P(), P()) + (owned,) * 8,
        check_vma=False,
    )
```

```python
import functools
import math

import jax
import jax.numpy as jnp
import numpy as np
from jax import lax
from jax.sharding import Mesh
from jax.sharding import PartitionSpec as P

WINDOW = 512
EPSILON = 1e-06
SQRT_HALF = 0.7071067811865476
BF = jnp.bfloat16
F32 = jnp.float32


def scaled_norm(values, gain_row):
    return (
        values * lax.rsqrt(jnp.mean(values * values, axis=-1, keepdims=True) + EPSILON) * gain_row
    )


def rotate(values, cosine, sine_part):
    half_dim = values.shape[-1] // 2
    first_half = values[..., :half_dim]
    second_half = values[..., half_dim:]
    return jnp.concatenate(
        [
            first_half * cosine - second_half * sine_part,
            second_half * cosine + first_half * sine_part,
        ],
        axis=-1,
    )


def rope_tables(positions, head_dim):
    half_dim = head_dim // 2
    frequency = jnp.exp(
        jnp.arange(half_dim, dtype=jnp.float32) * (-2.0 * math.log(10000.0) / head_dim)
    )
    phase_angle = positions.astype(jnp.float32)[:, None] * frequency[None, :]
    return (jnp.cos(phase_angle)[:, None, :], jnp.sin(phase_angle)[:, None, :])


def dot_plain(left_side, right_side):
    return jnp.dot(left_side, right_side, preferred_element_type=jnp.float32)


def dot_right_t(left_side, right_side):
    return lax.dot_general(
        left_side, right_side, (((1,), (1,)), ((), ())), preferred_element_type=jnp.float32
    )


def dot_left_t(left_side, right_side):
    return lax.dot_general(
        left_side, right_side, (((0,), (0,)), ((), ())), preferred_element_type=jnp.float32
    )


def gelu_tanh(values):
    return jax.nn.gelu(values, approximate=True)


def after(value, *others):
    return lax.optimization_barrier((value,) + others)[0]


def gelu_terms(gate, up):
    root = 0.7978845608
    square = gate * gate
    bend = jnp.tanh(root * (gate + 0.044715 * gate * square))
    half = 0.5 * (1.0 + bend)
    value = gate * half
    slope = half + 0.5 * gate * (1.0 - bend * bend) * root * (1.0 + 3.0 * 0.044715 * square)
    return value.astype(BF), (slope * up).astype(BF)


def swap(value, axis):
    return lax.ppermute(value, axis, [(0, 1), (1, 0)])


def place_on(axes):
    place = jnp.int32(0)
    for axis in axes:
        place = place * 2 + lax.axis_index(axis)
    return place


def combine(*values):
    total = values[0].astype(F32)
    for value in values[1:]:
        total = total + value.astype(F32)
    return total.astype(BF)


class Order:
    def __init__(self):
        self.last = ()

    def go(self, *values):
        return list(lax.optimization_barrier(values + self.last)[: len(values)])

    def mark(self, *values):
        self.last = tuple(values)
        return list(values)

    def put(self, value, axis):
        return Transfer(swap(value, axis))

    def wait(self, *transfers):
        for transfer, value in zip(
            transfers, self.mark(*self.go(*[transfer.value for transfer in transfers]))
        ):
            transfer.value = value


class Transfer:
    def __init__(self, value):
        self.value = value


class Gather:
    def __init__(self, value, axes, order):
        self.axes, self.order, self.value = axes, order, value
        self.sent = [order.put(value, axis) for axis in axes] if len(axes) == 2 else []
        self.first = self.sent

    def next(self):
        if len(self.axes) == 2:
            half = self.value.shape[0] // 2
            from_one, from_two = [transfer.value for transfer in self.sent]
            self.sent = [
                self.order.put(from_two[half:], self.axes[0]),
                self.order.put(from_one[:half], self.axes[1]),
            ]

    def near_blocks(self):
        return [self.value, self.first[1].value, self.first[0].value]

    def far_block(self):
        return jnp.concatenate([self.sent[1].value, self.sent[0].value], axis=0)

    def blocks(self):
        if len(self.axes) == 2:
            return self.near_blocks() + [self.far_block()]
        blocks = [self.value]
        for axis in reversed(self.axes):
            blocks = blocks + [swap(block, axis) for block in blocks]
        return blocks


class Scatter:
    def __init__(self, parts, axes, order):
        self.parts, self.axes, self.order = parts, axes, order
        self.half = parts[0].shape[0] // 2
        self.sent = []
        if len(axes) == 2:
            self.sent = [
                order.put(parts[3][self.half :], axes[0]),
                order.put(parts[3][: self.half], axes[1]),
            ]

    def next(self):
        if len(self.axes) == 2:
            half, (own, one, two, far) = self.half, self.parts
            via_two, via_one = [transfer.value for transfer in self.sent]
            two = jnp.concatenate([combine(two[:half], via_one), two[half:]], axis=0)
            one = jnp.concatenate([one[:half], combine(one[half:], via_two)], axis=0)
            self.sent = [self.order.put(two, self.axes[0]), self.order.put(one, self.axes[1])]

    def total(self):
        parts = self.parts
        if len(self.axes) != 2:
            for axis in self.axes:
                half = len(parts) // 2
                parts = [
                    combine(mine, swap(theirs, axis))
                    for mine, theirs in zip(parts[:half], parts[half:])
                ]
            return parts[0].astype(F32)
        total = parts[0].astype(F32)
        for transfer in self.sent:
            total = total + transfer.value.astype(F32)
        return total


def reorder(blocks, axes):
    count = len(axes)
    for bit, axis in enumerate(reversed(axes)):
        flip = lax.axis_index(axis) == 1
        blocks = [jnp.where(flip, blocks[k ^ (1 << bit)], blocks[k]) for k in range(1 << count)]
    return blocks


def stack_pair(mine, other, axis, dim):
    first = lax.axis_index(axis) == 0
    return jnp.stack([jnp.where(first, mine, other), jnp.where(first, other, mine)], axis=dim)


def pick(value, which, dim=0):
    return lax.dynamic_index_in_dim(value, which, dim, keepdims=False)


def body(
    rep_axes,
    line_axes,
    hidden_in,
    layer_vectors,
    positions,
    cotangent,
    model_gains,
    head_gains,
    qkv_weight,
    out_weight,
    laurel_down,
    laurel_up,
    gate_up_weight,
    down_weight,
    layer_gate,
    layer_project,
):
    far_axes, near_axis = line_axes[:-1], line_axes[-1]
    team_axes = rep_axes
    shard_axes = line_axes + ("core",)
    tokens, width = hidden_in.shape
    head_dim = head_gains.shape[1]
    query_heads = out_weight.shape[1] // head_dim
    kv_heads = (qkv_weight.shape[1] // head_dim - query_heads) // 2
    group = query_heads // kv_heads
    ffn_units = down_weight.shape[1]
    rank = laurel_down.shape[1]
    score_scale = 1.0 / math.sqrt(head_dim)
    reps = 1 << len(rep_axes)
    line = 1 << len(line_axes)
    teams = 1 << len(far_axes)
    cores = 2
    core = lax.axis_index("core")
    rep = place_on(rep_axes)
    near = lax.axis_index(near_axis)
    weight_rows = qkv_weight.shape[0]
    group_width = group * head_dim
    kv_width = 2 * head_dim
    query_part = group_width // reps
    kv_part = kv_width // reps
    units = ffn_units // reps
    pair = 2 * tokens
    assert kv_heads == cores and pair >= WINDOW

    order = Order()
    go, mark, put, wait = order.go, order.mark, order.put, order.wait

    def waits(*transfers):
        wait(*[transfer for transfer in transfers if transfer is not None])

    def qkv_columns(c):
        key_start = query_heads * head_dim + c * head_dim
        value_start = (query_heads + kv_heads) * head_dim + c * head_dim
        offset = rep * kv_part
        kv_start = jnp.where(offset < head_dim, key_start + offset, value_start + offset - head_dim)
        return jnp.concatenate(
            [
                lax.dynamic_slice_in_dim(
                    qkv_weight, c * group_width + rep * query_part, query_part, 1
                ),
                lax.dynamic_slice_in_dim(qkv_weight, kv_start, kv_part, 1),
            ],
            axis=1,
        )

    def out_columns(c):
        return lax.dynamic_slice_in_dim(
            out_weight, c * group_width + rep * query_part, query_part, 1
        )

    attention_rows = jnp.concatenate(
        [qkv_columns(c) for c in range(cores)]
        + [out_columns(c) for c in range(cores)]
        + [laurel_down, laurel_up, layer_gate, layer_project],
        axis=1,
    )
    attention_whole = lax.all_gather(attention_rows, shard_axes, axis=0, tiled=True)
    part = query_part + kv_part
    qkv_own = lax.dynamic_slice_in_dim(attention_whole, core * part, part, 1)
    out_own = lax.dynamic_slice_in_dim(
        attention_whole, cores * part + core * query_part, query_part, 1
    )

    def ffn_rows(source, start):
        return lax.dynamic_slice_in_dim(source, start + rep * units, units, 1)

    ffn_mine = jnp.concatenate(
        [
            ffn_rows(gate_up_weight, 0),
            ffn_rows(gate_up_weight, ffn_units),
            ffn_rows(down_weight, 0),
        ],
        axis=1,
    )
    hidden_sent = put(hidden_in, "core")
    pos_sent = put(positions, "core")
    wait(hidden_sent, pos_sent)

    hidden_pair = jnp.concatenate([hidden_in, hidden_sent.value], axis=0)
    pos_pair = jnp.concatenate([positions, pos_sent.value], axis=0)
    steps = jnp.arange(tokens, dtype=jnp.int32)
    index = jnp.concatenate([core * tokens + steps, (1 - core) * tokens + steps])
    hidden_f = hidden_in.astype(F32)
    first_pair = scaled_norm(hidden_pair.astype(F32), model_gains[0]).astype(BF)
    normed_one, norm_one_pull = jax.vjp(scaled_norm, hidden_f, model_gains[0])
    cosine, sine_part = rope_tables(pos_pair, head_dim)
    first_pair, cosine, sine_part = mark(first_pair, cosine, sine_part)
    first_norm = first_pair[:tokens]
    ffn_mine, qkv_own, out_own = mark(*go(ffn_mine, qkv_own, out_own))
    ffn_whole = lax.all_gather(ffn_mine, shard_axes, axis=0, tiled=True)
    gate_up_cols = ffn_whole[:, : 2 * units]
    down_cols = ffn_whole[:, 2 * units :]
    qkv_gather = Gather(qkv_own, rep_axes, order)
    ple = layer_gate.shape[1]
    small_full = go(attention_whole)[0][:, cores * (part + query_part) :]
    down_low_full = small_full[:, :rank]
    up_low_full = small_full[:, rank : 2 * rank]
    gate_layer_full = small_full[:, 2 * rank : 2 * rank + ple]
    project_full = small_full[:, 2 * rank + ple :]
    middle = dot_plain(first_norm, down_low_full).astype(BF)
    side_pre, middle = mark(dot_right_t(middle, up_low_full), middle)
    waits(*qkv_gather.sent)
    qkv_gather.next()
    waits(*qkv_gather.sent)
    ordered_heads = query_part != head_dim

    def head_order(blocks):
        return reorder(blocks, rep_axes) if ordered_heads else blocks

    out_gather = Gather(go(out_own)[0], rep_axes, order)
    qkv_blocks = qkv_gather.blocks()
    (qkv_part,) = mark(
        jnp.concatenate(
            head_order([block[:, :query_part] for block in qkv_blocks])
            + reorder([block[:, query_part:] for block in qkv_blocks], rep_axes),
            axis=1,
        )
    )
    proj = dot_plain(first_pair, qkv_part)
    query_pre = proj[:, :group_width].reshape(pair, group, head_dim)
    key_pre = proj[:, group_width : group_width + head_dim].reshape(pair, 1, head_dim)
    value_own = proj[:, group_width + head_dim :].astype(BF)

    def prepare(query_in, key_in, query_gain, key_gain):
        return (
            rotate(scaled_norm(query_in, query_gain), cosine, sine_part),
            rotate(scaled_norm(key_in, key_gain), cosine, sine_part),
        )

    (query_rot, key_rot), prepare_pull = jax.vjp(
        prepare, query_pre, key_pre, head_gains[0], head_gains[1]
    )
    query_low = query_rot.astype(BF)
    own_keys = jnp.concatenate([key_rot.astype(BF).reshape(pair, head_dim), value_own], axis=1)
    own_keys, query_low = mark(own_keys, query_low)
    keys_sent = Transfer(
        lax.ppermute(own_keys, line_axes, [(i, i + 1) for i in range(line - 1)])
    )
    waits(keys_sent, *out_gather.sent)
    out_gather.next()
    earlier = keys_sent.value
    all_keys = jnp.concatenate([earlier, own_keys], axis=0)
    key_all = all_keys[:, :head_dim]
    value_all = all_keys[:, head_dim:]
    key_index = jnp.concatenate([index - pair, index])
    offsets = index[:, None] - key_index[None, :]
    valid_keys = (offsets >= 0) & (offsets < WINDOW) & (offsets <= pos_pair[:, None])

    def masked_scores():
        raw = jnp.einsum("qgd,kd->gqk", query_low, key_all, preferred_element_type=F32)
        return jnp.where(valid_keys, raw * score_scale, -1e30)

    scores = masked_scores()
    row_max = jnp.max(scores, axis=-1, keepdims=True)
    exponents = jnp.exp(scores - row_max)
    row_total = jnp.sum(exponents, axis=-1, keepdims=True)
    log_total = row_max + jnp.log(row_total)
    probs_low = (exponents / row_total).astype(BF)
    mixed = jnp.einsum("gqk,kd->qgd", probs_low, value_all, preferred_element_type=F32)
    (mixed_low,) = mark(mixed.reshape(pair, group_width).astype(BF))
    waits(*out_gather.sent)
    (out_part,) = mark(jnp.concatenate(head_order(out_gather.blocks()), axis=1))
    (attn_sum,) = mark(dot_right_t(mixed_low, out_part))
    attn_sent = put(attn_sum[tokens:], "core")
    wait(attn_sent)
    attn_pre = attn_sum[:tokens] + attn_sent.value
    attn_out, attn_pull = jax.vjp(scaled_norm, attn_pre, model_gains[1])
    side_out, side_pull = jax.vjp(scaled_norm, side_pre, model_gains[2])
    first_sum = (hidden_f + attn_out + first_norm.astype(F32) + side_out) * SQRT_HALF
    normed_two, norm_two_pull = jax.vjp(scaled_norm, first_sum, model_gains[3])
    second_norm, first_sum = mark(normed_two.astype(BF), first_sum)

    team = reps
    staged = team == 4
    groups = [[0], [1, 2], [3]] if staged else [list(range(team))]

    def group_of(blocks, g):
        return jnp.concatenate([blocks[k] for k in groups[g]], axis=0)

    def by_block(results):
        parts = [None] * team
        for group, result in zip(groups, results):
            for i, k in enumerate(group):
                parts[k] = result[i * tokens : (i + 1) * tokens]
        return parts

    def step_blocks(gather, g):
        if not staged:
            return group_of(gather.blocks(), 0)
        if g == 0:
            return gather.value
        if g == 1:
            return jnp.concatenate(gather.near_blocks()[1:], axis=0)
        return gather.far_block()

    second_gather = Gather(second_norm, team_axes, order)
    second_groups, gate_ups, hidden_groups, norm_groups = [], [], [], []

    def gate_step(g):
        second_groups.append(step_blocks(second_gather, g))
        (block,) = go(second_groups[-1])
        gate_up = dot_plain(block, gate_up_cols)
        hidden = (gelu_tanh(gate_up[:, :units]) * gate_up[:, units:]).astype(BF)
        gate_up, hidden = mark(gate_up, hidden)
        gate_ups.append(gate_up)
        hidden_groups.append(hidden)

    def down_step(g):
        (block,) = go(hidden_groups[g])
        norm_groups.extend(mark(dot_right_t(block, down_cols).astype(BF)))

    waits(*second_gather.sent)
    second_gather.next()
    waits(*second_gather.sent)
    first_gather = Gather(go(first_norm)[0], rep_axes, order)
    waits(*first_gather.sent)
    first_gather.next()
    waits(*first_gather.sent)
    first_others = jnp.stack(first_gather.blocks()[1:])
    first_sent = put(first_others, "core")
    wait(first_sent)
    (first_all,) = mark(
        jnp.concatenate(
            [first_pair]
            + [block for pair_blocks in zip(first_others, first_sent.value) for block in pair_blocks],
            axis=0,
        )
    )
    for g in range(len(groups)):
        gate_step(g)
    for g in range(len(groups)):
        down_step(g)
    ffn_scatter = Scatter(by_block(norm_groups), team_axes, order)
    second_all = jnp.concatenate(second_groups, axis=0)
    hidden_all = jnp.concatenate(hidden_groups, axis=0)
    second_all, hidden_all = mark(*go(second_all, hidden_all))
    waits(*ffn_scatter.sent)
    ffn_scatter.next()
    ffn_terms = []
    for gate_up in go(*gate_ups):
        ffn_terms.append(gelu_terms(gate_up[:, :units], gate_up[:, units:]))
    mark(*[term for terms in ffn_terms for term in terms])
    waits(*ffn_scatter.sent)
    (ffn_pre,) = mark(ffn_scatter.total())
    ffn_out, ffn_pull = jax.vjp(scaled_norm, ffn_pre, model_gains[4])
    second_sum = first_sum + ffn_out
    second_low = second_sum.astype(BF)
    ple_pre = dot_plain(second_low, gate_layer_full)

    def gate_vectors(pre_values, vector_values):
        return gelu_tanh(pre_values) * vector_values

    gated_val, gated_pull = jax.vjp(gate_vectors, ple_pre, layer_vectors.astype(F32))
    gated_low = gated_val.astype(BF)
    last_pre = dot_right_t(gated_low, project_full)
    last_out, last_pull = jax.vjp(scaled_norm, last_pre, model_gains[5])
    layer_out = (second_sum + last_out).astype(BF)

    upstream = cotangent.astype(F32)
    d_last, grad_gain_five = last_pull(upstream)
    d_last_low = d_last.astype(BF)
    d_gated = dot_plain(d_last_low, project_full)
    d_ple_pre, grad_vectors = gated_pull(d_gated)
    d_ple_low = d_ple_pre.astype(BF)
    d_second = upstream + dot_right_t(d_ple_low, gate_layer_full)
    d_ffn, grad_gain_four = ffn_pull(d_second)
    (d_ffn_low,) = mark(d_ffn.astype(BF))
    ple_terms = jnp.concatenate(
        [dot_left_t(second_low, d_ple_low), dot_left_t(d_last_low, gated_low)], axis=1
    ).astype(BF)
    ple_rows = lax.psum_scatter(ple_terms, shard_axes, scatter_dimension=0, tiled=True)
    d_ffn_gather = Gather(d_ffn_low, team_axes, order)
    d_ffn_groups, d_gate_groups, d_norm_groups = [], [], []

    def back_step(g):
        d_ffn_groups.append(step_blocks(d_ffn_gather, g))
        (block,) = go(d_ffn_groups[-1])
        value, slope = ffn_terms[g]
        d_hidden = dot_plain(block, down_cols)
        d_gate = (d_hidden * slope.astype(F32)).astype(BF)
        d_up = (d_hidden * value.astype(F32)).astype(BF)
        d_gate_groups.append(jnp.concatenate([d_gate, d_up], axis=1))
        d_norm = dot_right_t(d_gate_groups[-1], gate_up_cols).astype(BF)
        d_norm_groups.extend(mark(d_norm))

    if staged:
        back_step(0)
        waits(*d_ffn_gather.sent)
        d_ffn_gather.next()
        back_step(1)
        waits(*d_ffn_gather.sent)
        back_step(2)
    else:
        back_step(0)
    norm_scatter = Scatter(by_block(d_norm_groups), team_axes, order)

    def keep(value, axis, dim):
        return pick(value, lax.axis_index(axis), dim)

    def send(value, axis, dim):
        return put(pick(value, 1 - lax.axis_index(axis), dim), axis)

    def far_send(value):
        return send(value, far_axes[0], 0) if len(far_axes) == 1 else None

    def far_halve(value, transfer):
        if len(far_axes) == 1:
            return combine(keep(value, far_axes[0], 0), transfer.value)
        for axis in far_axes:
            value = value.reshape((2, value.shape[0] // 2) + value.shape[1:])
            value = combine(
                keep(value, axis, 0), swap(pick(value, 1 - lax.axis_index(axis), 0), axis)
            )
        return value

    class FfnGradient:
        def __init__(self, term):
            self.mine = lax.psum_scatter(term, shard_axes, scatter_dimension=0, tiled=True)

        def spread(self):
            self.gather = Gather(go(self.mine[:, :units])[0], rep_axes, order)

        def columns(self):
            blocks = reorder(go(*self.gather.blocks()), rep_axes)
            (whole,) = mark(jnp.concatenate([block.astype(F32) for block in blocks], axis=1))
            return whole

    (d_ffn_all,) = mark(jnp.concatenate(go(*d_ffn_groups), axis=0))
    (down_terms,) = mark(dot_left_t(d_ffn_all, hidden_all).astype(BF))
    down_terms, ple_rows = lax.optimization_barrier((down_terms, ple_rows))
    down_grad = FfnGradient(down_terms)
    waits(*norm_scatter.sent)
    norm_scatter.next()
    (d_gate_all,) = mark(jnp.concatenate(go(*d_gate_groups), axis=0))
    (gate_terms,) = mark(dot_left_t(second_all, d_gate_all[:, :units]).astype(BF))
    gate_grad = FfnGradient(gate_terms)
    waits(*norm_scatter.sent)
    d_second_norm = norm_scatter.total()
    d_first_part, grad_gain_three = norm_two_pull(d_second_norm)
    d_branch = (d_second + d_first_part) * SQRT_HALF
    d_attn, grad_gain_one = attn_pull(d_branch)
    d_attn_low, d_branch = mark(d_attn.astype(BF), d_branch)
    d_attn_sent = put(d_attn_low, "core")
    d_side, grad_gain_two = side_pull(go(d_branch)[0])
    d_side_low = d_side.astype(BF)
    d_middle_low = dot_plain(d_side_low, up_low_full).astype(BF)
    laurel_terms = jnp.concatenate(
        [dot_left_t(first_norm, d_middle_low), dot_left_t(d_side_low, middle)], axis=1
    ).astype(BF)
    d_middle_low, laurel_terms = mark(d_middle_low, laurel_terms)
    wait(d_attn_sent)
    d_attn_pair = jnp.concatenate([d_attn_low, d_attn_sent.value], axis=0)
    (d_mixed_low,) = mark(dot_plain(d_attn_pair, out_part).astype(BF))
    d_mixed_low = d_mixed_low.reshape(pair, group, head_dim)
    (out_term,) = mark(dot_left_t(go(d_attn_pair)[0], mixed_low).astype(BF))

    def columns(value):
        return jnp.split(value, reps, axis=1)

    out_scatter = Scatter(head_order(columns(go(out_term)[0])), rep_axes, order)
    probabilities = jnp.exp(masked_scores() - log_total)
    (d_mixed_low,) = go(d_mixed_low)
    d_probs = jnp.einsum("qgd,kd->gqk", d_mixed_low, value_all, preferred_element_type=F32)
    row_dot = jnp.sum(probabilities * d_probs, axis=-1, keepdims=True)
    (d_scores,) = mark((probabilities * (d_probs - row_dot)).astype(BF))
    waits(*out_scatter.sent)
    out_scatter.next()
    (d_scores,) = go(d_scores)
    d_values = jnp.einsum("gqk,qgd->kd", probs_low, d_mixed_low, preferred_element_type=F32)
    d_keys = (
        jnp.einsum("gqk,qgd->kd", d_scores, query_low, preferred_element_type=F32) * score_scale
    )
    (key_grads,) = mark(jnp.concatenate([d_keys, d_values], axis=1))
    returned = Transfer(
        lax.ppermute(
            key_grads[:pair].astype(BF), line_axes, [(i + 1, i) for i in range(line - 1)]
        )
    )
    d_queries = (
        jnp.einsum("gqk,kd->qgd", go(d_scores)[0], key_all, preferred_element_type=F32)
        * score_scale
    )
    (d_queries,) = mark(d_queries)
    down_grad.spread()
    (up_terms,) = mark(dot_left_t(go(second_all)[0], d_gate_all[:, units:]).astype(BF))
    up_grad = FfnGradient(up_terms)
    waits(returned, *out_scatter.sent)
    own_grads = key_grads[pair:] + returned.value.astype(F32)
    d_query_pre, d_key_pre, grad_query_gain, grad_key_gain = prepare_pull(
        (d_queries, own_grads[:, :head_dim].reshape(pair, 1, head_dim))
    )
    d_proj = jnp.concatenate(
        [
            d_query_pre.reshape(pair, group_width),
            d_key_pre.reshape(pair, head_dim),
            own_grads[:, head_dim:],
        ],
        axis=1,
    ).astype(BF)
    (d_proj,) = mark(d_proj)

    def rep_put(value, k):
        return Transfer(lax.ppermute(value, rep_axes, [(i, i ^ k) for i in range(reps)]))

    proj_parts = [
        jnp.concatenate([one, two], axis=1)
        for one, two in zip(
            head_order(columns(d_proj[:, :group_width])),
            reorder(columns(d_proj[:, group_width:]), rep_axes),
        )
    ]
    proj_sent = [rep_put(proj_parts[k], k) for k in range(1, reps)]
    (out_total,) = mark(out_scatter.total().astype(BF))
    (norm_sum,) = mark(dot_right_t(go(d_proj)[0], qkv_part))
    norm_sent = put(norm_sum[tokens:], "core")
    waits(*proj_sent, *down_grad.gather.sent)
    proj_all = jnp.concatenate([proj_parts[0]] + [part.value for part in proj_sent], axis=0)
    (qkv_total,) = mark(dot_left_t(first_all, go(proj_all)[0]).astype(BF))

    def core_columns(value):
        return [jnp.where(core == c, value, jnp.zeros_like(value)) for c in range(cores)]

    (attention_terms,) = mark(
        jnp.concatenate(
            core_columns(qkv_total) + core_columns(out_total) + [laurel_terms], axis=1
        )
    )
    attention_sum = lax.psum_scatter(
        attention_terms, shard_axes, scatter_dimension=0, tiled=True
    )
    down_grad.gather.next()
    wait(norm_sent)
    d_first_norm = (
        norm_sum[:tokens]
        + norm_sent.value
        + dot_right_t(d_middle_low, down_low_full)
        + d_branch
    )
    d_input_part, grad_gain_zero = norm_one_pull(d_first_norm)
    grad_hidden, grad_gain_zero = mark(d_branch + d_input_part, grad_gain_zero)
    model_part = jnp.stack(
        [
            grad_gain_zero,
            grad_gain_one,
            grad_gain_two,
            grad_gain_three,
            grad_gain_four,
            grad_gain_five,
        ]
    )
    head_part = jnp.stack([grad_query_gain, grad_key_gain])
    gains = jnp.concatenate([model_part.reshape(-1, head_dim), head_part], axis=0)
    gain_axes = rep_axes + line_axes + ("core",)

    def gain_put(pair_axes):
        if len(pair_axes) == 1:
            return [put(gains, pair_axes[0])]
        across = lax.ppermute(gains, pair_axes, [(i, 3 - i) for i in range(4)])
        return [put(gains, pair_axes[0]), put(gains, pair_axes[1]), Transfer(across)]

    def gain_sum(transfers):
        values = [transfer.value for transfer in transfers]
        if len(values) == 1:
            return gains + values[0]
        return (gains + values[0]) + (values[1] + values[2])

    gain_steps = [gain_axes[i : i + 2] for i in range(0, len(gain_axes), 2)]
    gain_sent = gain_put(gain_steps[0])
    small_sum = go(ple_rows)[0]
    small_sent = put(small_sum, rep_axes[0])
    waits(small_sent, *down_grad.gather.sent, *gain_sent)
    gate_grad.spread()
    gains = gain_sum(gain_sent)
    gain_sent = gain_put(gain_steps[1])
    for axis in rep_axes[1:]:
        small_sum = combine(small_sum, small_sent.value)
        small_sent = put(small_sum, axis)
    grad_down = down_grad.columns()
    waits(small_sent, *gate_grad.gather.sent, *gain_sent)
    gate_grad.gather.next()
    ple_sum = small_sum.astype(F32) + small_sent.value.astype(F32)
    gains = gain_sum(gain_sent)
    for step in gain_steps[2:-1]:
        gain_sent = gain_put(step)
        waits(*gain_sent)
        gains = gain_sum(gain_sent)
    gain_sent = gain_put(gain_steps[-1])
    waits(*gain_sent, *gate_grad.gather.sent)
    gains = gain_sum(gain_sent)
    gate_columns = gate_grad.columns()
    up_grad.spread()
    waits(*up_grad.gather.sent)
    up_grad.gather.next()
    (attention_sum,) = go(attention_sum)
    waits(*up_grad.gather.sent)
    attention_width = cores * (part + query_part)
    (attention_sum,) = go(attention_sum)
    attention_gather = Gather(attention_sum[:, :attention_width], rep_axes, order)
    laurel_sum = attention_sum[:, attention_width:]
    laurel_sent = put(laurel_sum, rep_axes[0])
    up_columns = up_grad.columns()
    waits(laurel_sent, *attention_gather.sent)
    attention_gather.next()
    for axis in rep_axes[1:]:
        laurel_sum = combine(laurel_sum, laurel_sent.value)
        laurel_sent = put(laurel_sum, axis)
    grad_gate_up = jnp.concatenate([gate_columns, up_columns], axis=1)
    (grad_gate_up,) = mark(*go(grad_gate_up))
    waits(laurel_sent, *attention_gather.sent)
    attention_blocks = reorder(attention_gather.blocks(), rep_axes)
    grad_qkv = jnp.concatenate(
        [
            block[:, c * part : c * part + query_part].astype(F32)
            for c in range(cores)
            for block in attention_blocks
        ]
        + [
            block[:, c * part + query_part : (c + 1) * part].astype(F32)
            for half in (attention_blocks[: reps // 2], attention_blocks[reps // 2 :])
            for c in range(cores)
            for block in half
        ],
        axis=1,
    )
    grad_out = jnp.concatenate(
        [
            block[:, cores * part + c * query_part : cores * part + (c + 1) * query_part].astype(
                F32
            )
            for c in range(cores)
            for block in attention_blocks
        ],
        axis=1,
    )
    laurel_sum = laurel_sum.astype(F32) + laurel_sent.value.astype(F32)
    grad_laurel_down, grad_laurel_up = laurel_sum[:, :rank], laurel_sum[:, rank:]
    grad_layer_gate, grad_layer_project = ple_sum[:, :ple], ple_sum[:, ple:]
    grad_model_gains = gains[: -head_part.shape[0]].reshape(model_part.shape)
    grad_head_gains = gains[-head_part.shape[0] :]
    return (
        layer_out,
        grad_hidden,
        grad_vectors,
        grad_model_gains,
        grad_head_gains,
        grad_qkv,
        grad_out,
        grad_laurel_down,
        grad_laurel_up,
        grad_gate_up,
        grad_down,
        grad_layer_gate,
        grad_layer_project,
    )


def solution(mesh):
    reps, shards = mesh.shape["rep"], mesh.shape["shard"]
    rep_axes = tuple(f"rep{i}" for i in range(reps.bit_length() - 1))
    line_axes = tuple(f"line{i}" for i in range(shards.bit_length() - 2))
    axes = rep_axes + line_axes + ("core",)
    assert 1 << len(axes) == reps * shards
    fine = Mesh(np.asarray(mesh.devices).reshape((2,) * len(axes)), axes)
    rows, owned = P(axes, None), P(line_axes + ("core",), None)
    return jax.shard_map(
        functools.partial(body, rep_axes, line_axes),
        mesh=fine,
        in_specs=(rows, rows, P(axes), rows, P(), P()) + (owned,) * 8,
        out_specs=(rows, rows, rows, P(), P()) + (owned,) * 8,
        check_vma=False,
    )
```

```python
import functools
import math

import jax
import jax.numpy as jnp
import numpy as np
from jax import lax
from jax.experimental import pallas as pl
from jax.experimental.pallas import tpu as pltpu
from jax.sharding import Mesh
from jax.sharding import PartitionSpec as P

WINDOW = 512
EPSILON = 1e-06
SQRT_HALF = 0.7071067811865476
BF = jnp.bfloat16
F32 = jnp.float32


def scaled_norm(values, gain_row):
    return (
        values * lax.rsqrt(jnp.mean(values * values, axis=-1, keepdims=True) + EPSILON) * gain_row
    )


def rotate(values, cosine, sine_part):
    half_dim = values.shape[-1] // 2
    first_half = values[..., :half_dim]
    second_half = values[..., half_dim:]
    return jnp.concatenate(
        [
            first_half * cosine - second_half * sine_part,
            second_half * cosine + first_half * sine_part,
        ],
        axis=-1,
    )


def rope_tables(positions, head_dim):
    half_dim = head_dim // 2
    frequency = jnp.exp(
        jnp.arange(half_dim, dtype=jnp.float32) * (-2.0 * math.log(10000.0) / head_dim)
    )
    phase_angle = positions.astype(jnp.float32)[:, None] * frequency[None, :]
    return (jnp.cos(phase_angle)[:, None, :], jnp.sin(phase_angle)[:, None, :])


def dot_plain(left_side, right_side):
    return jnp.dot(left_side, right_side, preferred_element_type=jnp.float32)


def dot_right_t(left_side, right_side):
    return lax.dot_general(
        left_side, right_side, (((1,), (1,)), ((), ())), preferred_element_type=jnp.float32
    )


def dot_left_t(left_side, right_side):
    return lax.dot_general(
        left_side, right_side, (((0,), (0,)), ((), ())), preferred_element_type=jnp.float32
    )


def terms_kernel(left_ref, right_ref, out_ref):
    out_ref[...] = dot_left_t(left_ref[...], right_ref[...]).astype(out_ref.dtype)


def gradient_terms(left_side, right_side, size, block):
    rows, columns = left_side.shape
    step = math.gcd(columns, 512)
    return pl.pallas_call(
        terms_kernel,
        grid=(columns // step,),
        in_specs=[
            pl.BlockSpec((rows, step), lambda i: (0, i)),
            pl.BlockSpec((rows, size), lambda i: (0, block)),
        ],
        out_specs=pl.BlockSpec((step, size), lambda i: (i, 0)),
        out_shape=jax.ShapeDtypeStruct((columns, size), BF),
        cost_estimate=pl.CostEstimate(flops=1, bytes_accessed=1, transcendentals=0),
        compiler_params=pltpu.CompilerParams(vmem_limit_bytes=40 * 1024 * 1024),
    )(left_side, right_side)


def gelu_tanh(values):
    return jax.nn.gelu(values, approximate=True)


def after(value, *others):
    return lax.optimization_barrier((value,) + others)[0]


def gelu_terms(gate, up):
    root = 0.7978845608
    square = gate * gate
    bend = jnp.tanh(root * (gate + 0.044715 * gate * square))
    half = 0.5 * (1.0 + bend)
    value = gate * half
    slope = half + 0.5 * gate * (1.0 - bend * bend) * root * (1.0 + 3.0 * 0.044715 * square)
    return value.astype(BF), (slope * up).astype(BF)


def swap(value, axis):
    return lax.ppermute(value, axis, [(0, 1), (1, 0)])


def place_on(axes):
    place = jnp.int32(0)
    for axis in axes:
        place = place * 2 + lax.axis_index(axis)
    return place


def combine(*values):
    total = values[0].astype(F32)
    for value in values[1:]:
        total = total + value.astype(F32)
    return total.astype(BF)


class Order:
    def __init__(self):
        self.last = ()

    def go(self, *values):
        return list(lax.optimization_barrier(values + self.last)[: len(values)])

    def mark(self, *values):
        self.last = tuple(values)
        return list(values)

    def put(self, value, axis):
        return Transfer(swap(value, axis))

    def wait(self, *transfers):
        for transfer, value in zip(
            transfers, self.mark(*self.go(*[transfer.value for transfer in transfers]))
        ):
            transfer.value = value


class Transfer:
    def __init__(self, value):
        self.value = value


class Gather:
    def __init__(self, value, axes, order):
        self.axes, self.order, self.value = axes, order, value
        self.sent = [order.put(value, axis) for axis in axes] if len(axes) == 2 else []
        self.first = self.sent

    def next(self):
        if len(self.axes) == 2:
            half = self.value.shape[0] // 2
            from_one, from_two = [transfer.value for transfer in self.sent]
            self.sent = [
                self.order.put(from_two[half:], self.axes[0]),
                self.order.put(from_one[:half], self.axes[1]),
            ]

    def near_blocks(self):
        return [self.value, self.first[1].value, self.first[0].value]

    def far_block(self):
        return jnp.concatenate([self.sent[1].value, self.sent[0].value], axis=0)

    def blocks(self):
        if len(self.axes) == 2:
            return self.near_blocks() + [self.far_block()]
        blocks = [self.value]
        for axis in reversed(self.axes):
            blocks = blocks + [swap(block, axis) for block in blocks]
        return blocks


class Scatter:
    def __init__(self, parts, axes, order):
        self.parts, self.axes, self.order = parts, axes, order
        self.half = parts[0].shape[0] // 2
        self.sent = []
        if len(axes) == 2:
            self.sent = [
                order.put(parts[3][self.half :], axes[0]),
                order.put(parts[3][: self.half], axes[1]),
            ]

    def next(self):
        if len(self.axes) == 2:
            half, (own, one, two, far) = self.half, self.parts
            via_two, via_one = [transfer.value for transfer in self.sent]
            two = jnp.concatenate([combine(two[:half], via_one), two[half:]], axis=0)
            one = jnp.concatenate([one[:half], combine(one[half:], via_two)], axis=0)
            self.sent = [self.order.put(two, self.axes[0]), self.order.put(one, self.axes[1])]

    def total(self):
        parts = self.parts
        if len(self.axes) != 2:
            for axis in self.axes:
                half = len(parts) // 2
                parts = [
                    combine(mine, swap(theirs, axis))
                    for mine, theirs in zip(parts[:half], parts[half:])
                ]
            return parts[0].astype(F32)
        total = parts[0].astype(F32)
        for transfer in self.sent:
            total = total + transfer.value.astype(F32)
        return total


def reorder(blocks, axes):
    count = len(axes)
    for bit, axis in enumerate(reversed(axes)):
        flip = lax.axis_index(axis) == 1
        blocks = [jnp.where(flip, blocks[k ^ (1 << bit)], blocks[k]) for k in range(1 << count)]
    return blocks


def stack_pair(mine, other, axis, dim):
    first = lax.axis_index(axis) == 0
    return jnp.stack([jnp.where(first, mine, other), jnp.where(first, other, mine)], axis=dim)


def pick(value, which, dim=0):
    return lax.dynamic_index_in_dim(value, which, dim, keepdims=False)


def body(
    rep_axes,
    line_axes,
    hidden_in,
    layer_vectors,
    positions,
    cotangent,
    model_gains,
    head_gains,
    qkv_weight,
    out_weight,
    laurel_down,
    laurel_up,
    gate_up_weight,
    down_weight,
    layer_gate,
    layer_project,
):
    far_axes, near_axis = line_axes[:-1], line_axes[-1]
    team_axes = rep_axes
    shard_axes = line_axes + ("core",)
    tokens, width = hidden_in.shape
    head_dim = head_gains.shape[1]
    query_heads = out_weight.shape[1] // head_dim
    kv_heads = (qkv_weight.shape[1] // head_dim - query_heads) // 2
    group = query_heads // kv_heads
    ffn_units = down_weight.shape[1]
    rank = laurel_down.shape[1]
    score_scale = 1.0 / math.sqrt(head_dim)
    reps = 1 << len(rep_axes)
    line = 1 << len(line_axes)
    teams = 1 << len(far_axes)
    cores = 2
    core = lax.axis_index("core")
    rep = place_on(rep_axes)
    near = lax.axis_index(near_axis)
    weight_rows = qkv_weight.shape[0]
    group_width = group * head_dim
    kv_width = 2 * head_dim
    query_part = group_width // reps
    kv_part = kv_width // reps
    units = ffn_units // reps
    pair = 2 * tokens
    assert kv_heads == cores and pair >= WINDOW

    order = Order()
    go, mark, put, wait = order.go, order.mark, order.put, order.wait

    def waits(*transfers):
        wait(*[transfer for transfer in transfers if transfer is not None])

    def qkv_columns(c):
        key_start = query_heads * head_dim + c * head_dim
        value_start = (query_heads + kv_heads) * head_dim + c * head_dim
        offset = rep * kv_part
        kv_start = jnp.where(offset < head_dim, key_start + offset, value_start + offset - head_dim)
        return jnp.concatenate(
            [
                lax.dynamic_slice_in_dim(
                    qkv_weight, c * group_width + rep * query_part, query_part, 1
                ),
                lax.dynamic_slice_in_dim(qkv_weight, kv_start, kv_part, 1),
            ],
            axis=1,
        )

    def out_columns(c):
        return lax.dynamic_slice_in_dim(
            out_weight, c * group_width + rep * query_part, query_part, 1
        )

    ple = layer_gate.shape[1]
    ple_part = ple // reps
    attention_rows = jnp.concatenate(
        [qkv_columns(c) for c in range(cores)]
        + [out_columns(c) for c in range(cores)]
        + [
            laurel_down,
            laurel_up,
            lax.dynamic_slice_in_dim(layer_gate, rep * ple_part, ple_part, 1),
            lax.dynamic_slice_in_dim(layer_project, rep * ple_part, ple_part, 1),
        ],
        axis=1,
    )
    attention_whole = lax.all_gather(attention_rows, shard_axes, axis=0, tiled=True)
    part = query_part + kv_part
    qkv_own = lax.dynamic_slice_in_dim(attention_whole, core * part, part, 1)
    out_own = lax.dynamic_slice_in_dim(
        attention_whole, cores * part + core * query_part, query_part, 1
    )

    def ffn_rows(source, start):
        return lax.dynamic_slice_in_dim(source, start + rep * units, units, 1)

    ffn_mine = jnp.concatenate(
        [
            ffn_rows(gate_up_weight, 0),
            ffn_rows(gate_up_weight, ffn_units),
            ffn_rows(down_weight, 0),
        ],
        axis=1,
    )
    hidden_sent = put(hidden_in, "core")
    pos_sent = put(positions, "core")
    wait(hidden_sent, pos_sent)

    hidden_pair = jnp.concatenate([hidden_in, hidden_sent.value], axis=0)
    pos_pair = jnp.concatenate([positions, pos_sent.value], axis=0)
    steps = jnp.arange(tokens, dtype=jnp.int32)
    index = jnp.concatenate([core * tokens + steps, (1 - core) * tokens + steps])
    hidden_f = hidden_in.astype(F32)
    first_pair = scaled_norm(hidden_pair.astype(F32), model_gains[0]).astype(BF)
    normed_one, norm_one_pull = jax.vjp(scaled_norm, hidden_f, model_gains[0])
    cosine, sine_part = rope_tables(pos_pair, head_dim)
    first_pair, cosine, sine_part = mark(first_pair, cosine, sine_part)
    first_norm = first_pair[:tokens]
    ffn_mine, qkv_own, out_own = mark(*go(ffn_mine, qkv_own, out_own))
    ffn_whole = lax.all_gather(ffn_mine, shard_axes, axis=0, tiled=True)
    gate_up_cols = ffn_whole[:, : 2 * units]
    down_cols = ffn_whole[:, 2 * units :]
    qkv_gather = Gather(qkv_own, rep_axes, order)
    small_full = go(attention_whole)[0][:, cores * (part + query_part) :]
    down_low_full = small_full[:, :rank]
    up_low_full = small_full[:, rank : 2 * rank]
    ple_own = small_full[:, 2 * rank :]
    middle = dot_plain(first_norm, down_low_full).astype(BF)
    side_pre, middle = mark(dot_right_t(middle, up_low_full), middle)
    waits(*qkv_gather.sent)
    qkv_gather.next()
    waits(*qkv_gather.sent)
    ordered_heads = query_part != head_dim

    def head_order(blocks):
        return reorder(blocks, rep_axes) if ordered_heads else blocks

    out_gather = Gather(go(out_own)[0], rep_axes, order)
    qkv_blocks = qkv_gather.blocks()
    (qkv_part,) = mark(
        jnp.concatenate(
            head_order([block[:, :query_part] for block in qkv_blocks])
            + reorder([block[:, query_part:] for block in qkv_blocks], rep_axes),
            axis=1,
        )
    )
    proj = dot_plain(first_pair, qkv_part)
    query_pre = proj[:, :group_width].reshape(pair, group, head_dim)
    key_pre = proj[:, group_width : group_width + head_dim].reshape(pair, 1, head_dim)
    value_own = proj[:, group_width + head_dim :].astype(BF)

    def prepare(query_in, key_in, query_gain, key_gain):
        return (
            rotate(scaled_norm(query_in, query_gain), cosine, sine_part),
            rotate(scaled_norm(key_in, key_gain), cosine, sine_part),
        )

    (query_rot, key_rot), prepare_pull = jax.vjp(
        prepare, query_pre, key_pre, head_gains[0], head_gains[1]
    )
    query_low = query_rot.astype(BF)
    own_keys = jnp.concatenate([key_rot.astype(BF).reshape(pair, head_dim), value_own], axis=1)
    own_keys, query_low = mark(own_keys, query_low)
    keys_sent = Transfer(
        lax.ppermute(own_keys, line_axes, [(i, i + 1) for i in range(line - 1)])
    )
    waits(keys_sent, *out_gather.sent)
    out_gather.next()
    earlier = keys_sent.value
    all_keys = jnp.concatenate([earlier, own_keys], axis=0)
    key_all = all_keys[:, :head_dim]
    value_all = all_keys[:, head_dim:]
    key_index = jnp.concatenate([index - pair, index])
    offsets = index[:, None] - key_index[None, :]
    valid_keys = (offsets >= 0) & (offsets < WINDOW) & (offsets <= pos_pair[:, None])

    def masked_scores():
        raw = jnp.einsum("qgd,kd->gqk", query_low, key_all, preferred_element_type=F32)
        return jnp.where(valid_keys, raw * score_scale, -1e30)

    scores = masked_scores()
    row_max = jnp.max(scores, axis=-1, keepdims=True)
    exponents = jnp.exp(scores - row_max)
    row_total = jnp.sum(exponents, axis=-1, keepdims=True)
    log_total = row_max + jnp.log(row_total)
    probs_low = (exponents / row_total).astype(BF)
    mixed = jnp.einsum("gqk,kd->qgd", probs_low, value_all, preferred_element_type=F32)
    (mixed_low,) = mark(mixed.reshape(pair, group_width).astype(BF))
    waits(*out_gather.sent)
    (out_part,) = mark(jnp.concatenate(head_order(out_gather.blocks()), axis=1))
    (attn_sum,) = mark(dot_right_t(mixed_low, out_part))
    attn_sent = put(attn_sum[tokens:], "core")
    wait(attn_sent)
    attn_pre = attn_sum[:tokens] + attn_sent.value
    attn_out, attn_pull = jax.vjp(scaled_norm, attn_pre, model_gains[1])
    side_out, side_pull = jax.vjp(scaled_norm, side_pre, model_gains[2])
    first_sum = (hidden_f + attn_out + first_norm.astype(F32) + side_out) * SQRT_HALF
    normed_two, norm_two_pull = jax.vjp(scaled_norm, first_sum, model_gains[3])
    second_norm, first_sum = mark(normed_two.astype(BF), first_sum)

    team = reps
    staged = team == 4
    groups = [[0], [1, 2], [3]] if staged else [list(range(team))]

    def group_of(blocks, g):
        return jnp.concatenate([blocks[k] for k in groups[g]], axis=0)

    def by_block(results):
        parts = [None] * team
        for group, result in zip(groups, results):
            for i, k in enumerate(group):
                parts[k] = result[i * tokens : (i + 1) * tokens]
        return parts

    def step_blocks(gather, g):
        if not staged:
            return group_of(gather.blocks(), 0)
        if g == 0:
            return gather.value
        if g == 1:
            return jnp.concatenate(gather.near_blocks()[1:], axis=0)
        return gather.far_block()

    second_gather = Gather(second_norm, team_axes, order)
    waits(*second_gather.sent)
    second_gather.next()
    waits(*second_gather.sent)
    first_gather = Gather(go(first_norm)[0], rep_axes, order)
    ple_gather = Gather(go(ple_own)[0], rep_axes, order)
    waits(*first_gather.sent, *ple_gather.sent)
    first_gather.next()
    ple_gather.next()
    waits(*first_gather.sent, *ple_gather.sent)
    ple_blocks = reorder(ple_gather.blocks(), rep_axes)
    gate_layer_full, project_full = mark(
        jnp.concatenate([block[:, :ple_part] for block in ple_blocks], axis=1),
        jnp.concatenate([block[:, ple_part:] for block in ple_blocks], axis=1),
    )
    first_others = jnp.stack(first_gather.blocks()[1:])
    first_sent = put(first_others, "core")
    wait(first_sent)
    (first_all,) = mark(
        jnp.concatenate(
            [first_pair]
            + [block for pair_blocks in zip(first_others, first_sent.value) for block in pair_blocks],
            axis=0,
        )
    )
    (second_all,) = mark(jnp.concatenate(go(*second_gather.blocks()), axis=0))
    gate_up = dot_plain(second_all, gate_up_cols)
    hidden_all = (gelu_tanh(gate_up[:, :units]) * gate_up[:, units:]).astype(BF)
    gate_up, hidden_all = mark(gate_up, hidden_all)
    (norm_all,) = mark(dot_right_t(hidden_all, down_cols).astype(BF))
    ffn_scatter = Scatter(
        [norm_all[k * tokens : (k + 1) * tokens] for k in range(team)], team_axes, order
    )
    waits(*ffn_scatter.sent)
    ffn_scatter.next()
    (gate_up,) = go(gate_up)
    ffn_value, ffn_slope = mark(*gelu_terms(gate_up[:, :units], gate_up[:, units:]))
    waits(*ffn_scatter.sent)
    (ffn_pre,) = mark(ffn_scatter.total())
    ffn_out, ffn_pull = jax.vjp(scaled_norm, ffn_pre, model_gains[4])
    second_sum = first_sum + ffn_out
    second_low = second_sum.astype(BF)
    ple_pre = dot_plain(second_low, gate_layer_full)

    def gate_vectors(pre_values, vector_values):
        return gelu_tanh(pre_values) * vector_values

    gated_val, gated_pull = jax.vjp(gate_vectors, ple_pre, layer_vectors.astype(F32))
    gated_low = gated_val.astype(BF)
    last_pre = dot_right_t(gated_low, project_full)
    last_out, last_pull = jax.vjp(scaled_norm, last_pre, model_gains[5])
    layer_out = (second_sum + last_out).astype(BF)

    upstream = cotangent.astype(F32)
    d_last, grad_gain_five = last_pull(upstream)
    d_last_low = d_last.astype(BF)
    d_gated = dot_plain(d_last_low, project_full)
    d_ple_pre, grad_vectors = gated_pull(d_gated)
    d_ple_low = d_ple_pre.astype(BF)
    d_second = upstream + dot_right_t(d_ple_low, gate_layer_full)
    d_ffn, grad_gain_four = ffn_pull(d_second)
    (d_ffn_low,) = mark(d_ffn.astype(BF))
    ple_terms = jnp.concatenate(
        [dot_left_t(second_low, d_ple_low), dot_left_t(d_last_low, gated_low)], axis=1
    ).astype(BF)
    ple_rows = lax.psum_scatter(ple_terms, shard_axes, scatter_dimension=0, tiled=True)
    d_ffn_gather = Gather(d_ffn_low, team_axes, order)
    d_ffn_groups, d_gate_groups, d_norm_groups = [], [], []

    def back_step(g):
        d_ffn_groups.append(step_blocks(d_ffn_gather, g))
        (block,) = go(d_ffn_groups[-1])
        at = sum(len(group) for group in groups[:g]) * tokens
        rows = slice(at, at + len(groups[g]) * tokens)
        value, slope = ffn_value[rows], ffn_slope[rows]
        d_hidden = dot_plain(block, down_cols)
        d_gate = (d_hidden * slope.astype(F32)).astype(BF)
        d_up = (d_hidden * value.astype(F32)).astype(BF)
        d_gate_groups.append(jnp.concatenate([d_gate, d_up], axis=1))
        d_norm = dot_right_t(d_gate_groups[-1], gate_up_cols).astype(BF)
        d_norm_groups.extend(mark(d_norm))

    if staged:
        waits(*d_ffn_gather.sent)
        d_ffn_gather.next()
        back_step(0)
        waits(*d_ffn_gather.sent)
    (d_ffn_all,) = mark(jnp.concatenate(go(*d_ffn_gather.blocks()), axis=0))
    (down_terms,) = mark(gradient_terms(d_ffn_all, hidden_all, units, 0))
    for g in range(1 if staged else 0, len(groups)):
        back_step(g)
    norm_scatter = Scatter(by_block(d_norm_groups), team_axes, order)

    def keep(value, axis, dim):
        return pick(value, lax.axis_index(axis), dim)

    def send(value, axis, dim):
        return put(pick(value, 1 - lax.axis_index(axis), dim), axis)

    def far_send(value):
        return send(value, far_axes[0], 0) if len(far_axes) == 1 else None

    def far_halve(value, transfer):
        if len(far_axes) == 1:
            return combine(keep(value, far_axes[0], 0), transfer.value)
        for axis in far_axes:
            value = value.reshape((2, value.shape[0] // 2) + value.shape[1:])
            value = combine(
                keep(value, axis, 0), swap(pick(value, 1 - lax.axis_index(axis), 0), axis)
            )
        return value

    class FfnGradient:
        def __init__(self, term):
            self.mine = lax.psum_scatter(term, shard_axes, scatter_dimension=0, tiled=True)

        def spread(self):
            self.gather = Gather(go(self.mine)[0], rep_axes, order)

        def place(self, whole, blocks, first, start=0):
            for k, block in enumerate(go(*blocks), first):
                whole = lax.dynamic_update_slice(
                    whole, block.astype(F32), (0, start + rep_of(k) * units)
                )
            return mark(whole)[0]

    def rep_of(k):
        return rep ^ k

    down_terms, ple_rows = lax.optimization_barrier((down_terms, ple_rows))
    down_grad = FfnGradient(down_terms)
    waits(*norm_scatter.sent)
    norm_scatter.next()
    (d_gate_all,) = mark(jnp.concatenate(go(*d_gate_groups), axis=0))
    (gate_terms,) = mark(gradient_terms(second_all, d_gate_all, units, 0))
    gate_grad = FfnGradient(gate_terms)
    (up_terms,) = mark(gradient_terms(go(second_all)[0], d_gate_all, units, 1))
    up_grad = FfnGradient(up_terms)
    waits(*norm_scatter.sent)
    d_second_norm = norm_scatter.total()
    d_first_part, grad_gain_three = norm_two_pull(d_second_norm)
    d_branch = (d_second + d_first_part) * SQRT_HALF
    d_attn, grad_gain_one = attn_pull(d_branch)
    d_attn_low, d_branch = mark(d_attn.astype(BF), d_branch)
    d_attn_sent = put(d_attn_low, "core")
    d_side, grad_gain_two = side_pull(go(d_branch)[0])
    d_side_low = d_side.astype(BF)
    d_middle_low = dot_plain(d_side_low, up_low_full).astype(BF)
    laurel_terms = jnp.concatenate(
        [dot_left_t(first_norm, d_middle_low), dot_left_t(d_side_low, middle)], axis=1
    ).astype(BF)
    d_middle_low, laurel_terms = mark(d_middle_low, laurel_terms)
    wait(d_attn_sent)
    d_attn_pair = jnp.concatenate([d_attn_low, d_attn_sent.value], axis=0)
    (d_mixed_low,) = mark(dot_plain(d_attn_pair, out_part).astype(BF))
    d_mixed_low = d_mixed_low.reshape(pair, group, head_dim)
    (out_term,) = mark(dot_left_t(go(d_attn_pair)[0], mixed_low).astype(BF))

    def columns(value):
        return jnp.split(value, reps, axis=1)

    out_scatter = Scatter(head_order(columns(go(out_term)[0])), rep_axes, order)
    probabilities = jnp.exp(masked_scores() - log_total)
    (d_mixed_low,) = go(d_mixed_low)
    d_probs = jnp.einsum("qgd,kd->gqk", d_mixed_low, value_all, preferred_element_type=F32)
    row_dot = jnp.sum(probabilities * d_probs, axis=-1, keepdims=True)
    (d_scores,) = mark((probabilities * (d_probs - row_dot)).astype(BF))
    small_sum = go(ple_rows)[0]
    small_sent = put(small_sum, rep_axes[0])
    waits(small_sent, *out_scatter.sent)
    out_scatter.next()
    for axis in rep_axes[1:]:
        small_sum = combine(small_sum, small_sent.value)
        small_sent = put(small_sum, axis)
    (d_scores,) = go(d_scores)
    d_values = jnp.einsum("gqk,qgd->kd", probs_low, d_mixed_low, preferred_element_type=F32)
    d_keys = (
        jnp.einsum("gqk,qgd->kd", d_scores, query_low, preferred_element_type=F32) * score_scale
    )
    (key_grads,) = mark(jnp.concatenate([d_keys, d_values], axis=1))
    returned = Transfer(
        lax.ppermute(
            key_grads[:pair].astype(BF), line_axes, [(i + 1, i) for i in range(line - 1)]
        )
    )
    d_queries = (
        jnp.einsum("gqk,kd->qgd", go(d_scores)[0], key_all, preferred_element_type=F32)
        * score_scale
    )
    (d_queries,) = mark(d_queries)
    down_grad.spread()
    waits(returned, small_sent, *out_scatter.sent, *down_grad.gather.sent)
    ple_sum = small_sum.astype(F32) + small_sent.value.astype(F32)
    own_grads = key_grads[pair:] + returned.value.astype(F32)
    d_query_pre, d_key_pre, grad_query_gain, grad_key_gain = prepare_pull(
        (d_queries, own_grads[:, :head_dim].reshape(pair, 1, head_dim))
    )
    d_proj = jnp.concatenate(
        [
            d_query_pre.reshape(pair, group_width),
            d_key_pre.reshape(pair, head_dim),
            own_grads[:, head_dim:],
        ],
        axis=1,
    ).astype(BF)
    (d_proj,) = mark(d_proj)

    def rep_put(value, k):
        return Transfer(lax.ppermute(value, rep_axes, [(i, i ^ k) for i in range(reps)]))

    proj_parts = [
        jnp.concatenate([one, two], axis=1)
        for one, two in zip(
            head_order(columns(d_proj[:, :group_width])),
            reorder(columns(d_proj[:, group_width:]), rep_axes),
        )
    ]
    proj_sent = [rep_put(proj_parts[k], k) for k in range(1, reps)]
    down_grad.gather.next()
    (out_total,) = mark(out_scatter.total().astype(BF))
    waits(*proj_sent, *down_grad.gather.sent)
    proj_all = jnp.concatenate([proj_parts[0]] + [part.value for part in proj_sent], axis=0)
    (qkv_total,) = mark(dot_left_t(first_all, go(proj_all)[0]).astype(BF))

    def core_columns(value):
        return [jnp.where(core == c, value, jnp.zeros_like(value)) for c in range(cores)]

    (attention_terms,) = mark(
        jnp.concatenate(
            core_columns(qkv_total) + core_columns(out_total) + [laurel_terms], axis=1
        )
    )
    attention_sum = lax.psum_scatter(
        attention_terms, shard_axes, scatter_dimension=0, tiled=True
    )
    gate_grad.spread()
    (norm_sum,) = mark(dot_right_t(go(d_proj)[0], qkv_part))
    norm_sent = put(norm_sum[tokens:], "core")
    wait(norm_sent)
    d_first_norm = (
        norm_sum[:tokens]
        + norm_sent.value
        + dot_right_t(d_middle_low, down_low_full)
        + d_branch
    )
    d_input_part, grad_gain_zero = norm_one_pull(d_first_norm)
    grad_hidden, grad_gain_zero = mark(d_branch + d_input_part, grad_gain_zero)
    model_part = jnp.stack(
        [
            grad_gain_zero,
            grad_gain_one,
            grad_gain_two,
            grad_gain_three,
            grad_gain_four,
            grad_gain_five,
        ]
    )
    head_part = jnp.stack([grad_query_gain, grad_key_gain])
    gains = jnp.concatenate([model_part.reshape(-1, head_dim), head_part], axis=0)
    gain_axes = rep_axes + line_axes + ("core",)

    def gain_put(pair_axes):
        if len(pair_axes) == 1:
            return [put(gains, pair_axes[0])]
        across = lax.ppermute(gains, pair_axes, [(i, 3 - i) for i in range(4)])
        return [put(gains, pair_axes[0]), put(gains, pair_axes[1]), Transfer(across)]

    def gain_sum(transfers):
        values = [transfer.value for transfer in transfers]
        if len(values) == 1:
            return gains + values[0]
        return (gains + values[0]) + (values[1] + values[2])

    gain_steps = [gain_axes[i : i + 2] for i in range(0, len(gain_axes), 2)]
    gain_sent = gain_put(gain_steps[0])
    grad_down = jnp.zeros((weight_rows, ffn_units), F32)
    grad_down = down_grad.place(grad_down, down_grad.gather.blocks(), 0)
    waits(*gain_sent, *gate_grad.gather.sent)
    gate_grad.gather.next()
    gains = gain_sum(gain_sent)
    gain_sent = gain_put(gain_steps[1])
    waits(*gain_sent, *gate_grad.gather.sent)
    up_grad.spread()
    gains = gain_sum(gain_sent)
    for step in gain_steps[2:-1]:
        gain_sent = gain_put(step)
        waits(*gain_sent)
        gains = gain_sum(gain_sent)
    gain_sent = gain_put(gain_steps[-1])
    grad_gate_up = jnp.zeros((weight_rows, 2 * ffn_units), F32)
    grad_gate_up = gate_grad.place(grad_gate_up, gate_grad.gather.blocks(), 0)
    waits(*gain_sent, *up_grad.gather.sent)
    up_grad.gather.next()
    gains = gain_sum(gain_sent)
    if staged:
        grad_gate_up = up_grad.place(grad_gate_up, up_grad.gather.near_blocks(), 0, ffn_units)
    waits(*up_grad.gather.sent)
    if staged:
        far_block = [up_grad.gather.far_block()]
        grad_gate_up = up_grad.place(grad_gate_up, far_block, 3, ffn_units)
    else:
        grad_gate_up = up_grad.place(grad_gate_up, up_grad.gather.blocks(), 0, ffn_units)
    (attention_sum,) = go(attention_sum)
    attention_width = cores * (part + query_part)
    attention_gather = Gather(attention_sum[:, :attention_width], rep_axes, order)
    laurel_sum = attention_sum[:, attention_width:]
    laurel_sent = put(laurel_sum, rep_axes[0])
    waits(laurel_sent, *attention_gather.sent)
    attention_gather.next()
    for axis in rep_axes[1:]:
        laurel_sum = combine(laurel_sum, laurel_sent.value)
        laurel_sent = put(laurel_sum, axis)
    waits(laurel_sent, *attention_gather.sent)
    attention_blocks = reorder(attention_gather.blocks(), rep_axes)
    grad_qkv = jnp.concatenate(
        [
            block[:, c * part : c * part + query_part].astype(F32)
            for c in range(cores)
            for block in attention_blocks
        ]
        + [
            block[:, c * part + query_part : (c + 1) * part].astype(F32)
            for half in (attention_blocks[: reps // 2], attention_blocks[reps // 2 :])
            for c in range(cores)
            for block in half
        ],
        axis=1,
    )
    grad_out = jnp.concatenate(
        [
            block[:, cores * part + c * query_part : cores * part + (c + 1) * query_part].astype(
                F32
            )
            for c in range(cores)
            for block in attention_blocks
        ],
        axis=1,
    )
    laurel_sum = laurel_sum.astype(F32) + laurel_sent.value.astype(F32)
    grad_laurel_down, grad_laurel_up = laurel_sum[:, :rank], laurel_sum[:, rank:]
    grad_layer_gate, grad_layer_project = ple_sum[:, :ple], ple_sum[:, ple:]
    grad_model_gains = gains[: -head_part.shape[0]].reshape(model_part.shape)
    grad_head_gains = gains[-head_part.shape[0] :]
    return (
        layer_out,
        grad_hidden,
        grad_vectors,
        grad_model_gains,
        grad_head_gains,
        grad_qkv,
        grad_out,
        grad_laurel_down,
        grad_laurel_up,
        grad_gate_up,
        grad_down,
        grad_layer_gate,
        grad_layer_project,
    )


def solution(mesh):
    reps, shards = mesh.shape["rep"], mesh.shape["shard"]
    rep_axes = tuple(f"rep{i}" for i in range(reps.bit_length() - 1))
    line_axes = tuple(f"line{i}" for i in range(shards.bit_length() - 2))
    axes = rep_axes + line_axes + ("core",)
    assert 1 << len(axes) == reps * shards
    fine = Mesh(np.asarray(mesh.devices).reshape((2,) * len(axes)), axes)
    rows, owned = P(axes, None), P(line_axes + ("core",), None)
    return jax.shard_map(
        functools.partial(body, rep_axes, line_axes),
        mesh=fine,
        in_specs=(rows, rows, P(axes), rows, P(), P()) + (owned,) * 8,
        out_specs=(rows, rows, rows, P(), P()) + (owned,) * 8,
        check_vma=False,
    )
```

```python
import functools
import math

import jax
import jax.numpy as jnp
import numpy as np
from jax import lax
from jax.experimental import pallas as pl
from jax.experimental.pallas import tpu as pltpu
from jax.sharding import Mesh
from jax.sharding import PartitionSpec as P

WINDOW = 512
EPSILON = 1e-06
SQRT_HALF = 0.7071067811865476
BF = jnp.bfloat16
F32 = jnp.float32


def scaled_norm(values, gain_row):
    return (
        values * lax.rsqrt(jnp.mean(values * values, axis=-1, keepdims=True) + EPSILON) * gain_row
    )


def rotate(values, cosine, sine_part):
    half_dim = values.shape[-1] // 2
    first_half = values[..., :half_dim]
    second_half = values[..., half_dim:]
    return jnp.concatenate(
        [
            first_half * cosine - second_half * sine_part,
            second_half * cosine + first_half * sine_part,
        ],
        axis=-1,
    )


def rope_tables(positions, head_dim):
    half_dim = head_dim // 2
    frequency = jnp.exp(
        jnp.arange(half_dim, dtype=jnp.float32) * (-2.0 * math.log(10000.0) / head_dim)
    )
    phase_angle = positions.astype(jnp.float32)[:, None] * frequency[None, :]
    return (jnp.cos(phase_angle)[:, None, :], jnp.sin(phase_angle)[:, None, :])


def dot_plain(left_side, right_side):
    return jnp.dot(left_side, right_side, preferred_element_type=jnp.float32)


def dot_right_t(left_side, right_side):
    return lax.dot_general(
        left_side, right_side, (((1,), (1,)), ((), ())), preferred_element_type=jnp.float32
    )


def dot_left_t(left_side, right_side):
    return lax.dot_general(
        left_side, right_side, (((0,), (0,)), ((), ())), preferred_element_type=jnp.float32
    )


def terms_kernel(left_ref, right_ref, out_ref):
    out_ref[...] = dot_left_t(left_ref[...], right_ref[...]).astype(out_ref.dtype)


def gradient_terms(left_side, right_side, size, block):
    rows, columns = left_side.shape
    step = math.gcd(columns, 512)
    return pl.pallas_call(
        terms_kernel,
        grid=(columns // step,),
        in_specs=[
            pl.BlockSpec((rows, step), lambda i: (0, i)),
            pl.BlockSpec((rows, size), lambda i: (0, block)),
        ],
        out_specs=pl.BlockSpec((step, size), lambda i: (i, 0)),
        out_shape=jax.ShapeDtypeStruct((columns, size), BF),
        cost_estimate=pl.CostEstimate(flops=1, bytes_accessed=1, transcendentals=0),
        compiler_params=pltpu.CompilerParams(vmem_limit_bytes=40 * 1024 * 1024),
    )(left_side, right_side)


def gelu_tanh(values):
    return jax.nn.gelu(values, approximate=True)


def after(value, *others):
    return lax.optimization_barrier((value,) + others)[0]


def gelu_terms(gate, up):
    root = 0.7978845608
    square = gate * gate
    bend = jnp.tanh(root * (gate + 0.044715 * gate * square))
    half = 0.5 * (1.0 + bend)
    value = gate * half
    slope = half + 0.5 * gate * (1.0 - bend * bend) * root * (1.0 + 3.0 * 0.044715 * square)
    return value.astype(BF), (slope * up).astype(BF)


def swap(value, axis):
    return lax.ppermute(value, axis, [(0, 1), (1, 0)])


def place_on(axes):
    place = jnp.int32(0)
    for axis in axes:
        place = place * 2 + lax.axis_index(axis)
    return place


def combine(*values):
    total = values[0].astype(F32)
    for value in values[1:]:
        total = total + value.astype(F32)
    return total.astype(BF)


class Order:
    def __init__(self):
        self.last = ()

    def go(self, *values):
        return list(lax.optimization_barrier(values + self.last)[: len(values)])

    def mark(self, *values):
        self.last = tuple(values)
        return list(values)

    def put(self, value, axis):
        return Transfer(swap(value, axis))

    def wait(self, *transfers):
        for transfer, value in zip(
            transfers, self.mark(*self.go(*[transfer.value for transfer in transfers]))
        ):
            transfer.value = value


class Transfer:
    def __init__(self, value):
        self.value = value


class Gather:
    def __init__(self, value, axes, order):
        self.axes, self.order, self.value = axes, order, value
        self.sent = [order.put(value, axis) for axis in axes] if len(axes) == 2 else []
        self.first = self.sent

    def next(self):
        if len(self.axes) == 2:
            half = self.value.shape[0] // 2
            from_one, from_two = [transfer.value for transfer in self.sent]
            self.sent = [
                self.order.put(from_two[half:], self.axes[0]),
                self.order.put(from_one[:half], self.axes[1]),
            ]

    def near_blocks(self):
        return [self.value, self.first[1].value, self.first[0].value]

    def far_block(self):
        return jnp.concatenate([self.sent[1].value, self.sent[0].value], axis=0)

    def blocks(self):
        if len(self.axes) == 2:
            return self.near_blocks() + [self.far_block()]
        blocks = [self.value]
        for axis in reversed(self.axes):
            blocks = blocks + [swap(block, axis) for block in blocks]
        return blocks


class Scatter:
    def __init__(self, parts, axes, order):
        self.parts, self.axes, self.order = parts, axes, order
        self.half = parts[0].shape[0] // 2
        self.sent = []
        if len(axes) == 2:
            self.sent = [
                order.put(parts[3][self.half :], axes[0]),
                order.put(parts[3][: self.half], axes[1]),
            ]

    def next(self):
        if len(self.axes) == 2:
            half, (own, one, two, far) = self.half, self.parts
            via_two, via_one = [transfer.value for transfer in self.sent]
            two = jnp.concatenate([combine(two[:half], via_one), two[half:]], axis=0)
            one = jnp.concatenate([one[:half], combine(one[half:], via_two)], axis=0)
            self.sent = [self.order.put(two, self.axes[0]), self.order.put(one, self.axes[1])]

    def total(self):
        parts = self.parts
        if len(self.axes) != 2:
            for axis in self.axes:
                half = len(parts) // 2
                parts = [
                    combine(mine, swap(theirs, axis))
                    for mine, theirs in zip(parts[:half], parts[half:])
                ]
            return parts[0].astype(F32)
        total = parts[0].astype(F32)
        for transfer in self.sent:
            total = total + transfer.value.astype(F32)
        return total


def reorder(blocks, axes):
    count = len(axes)
    for bit, axis in enumerate(reversed(axes)):
        flip = lax.axis_index(axis) == 1
        blocks = [jnp.where(flip, blocks[k ^ (1 << bit)], blocks[k]) for k in range(1 << count)]
    return blocks


def stack_pair(mine, other, axis, dim):
    first = lax.axis_index(axis) == 0
    return jnp.stack([jnp.where(first, mine, other), jnp.where(first, other, mine)], axis=dim)


def pick(value, which, dim=0):
    return lax.dynamic_index_in_dim(value, which, dim, keepdims=False)


def body(
    rep_axes,
    line_axes,
    hidden_in,
    layer_vectors,
    positions,
    cotangent,
    model_gains,
    head_gains,
    qkv_weight,
    out_weight,
    laurel_down,
    laurel_up,
    gate_up_weight,
    down_weight,
    layer_gate,
    layer_project,
):
    far_axes, near_axis = line_axes[:-1], line_axes[-1]
    team_axes = rep_axes
    shard_axes = line_axes + ("core",)
    tokens, width = hidden_in.shape
    head_dim = head_gains.shape[1]
    query_heads = out_weight.shape[1] // head_dim
    kv_heads = (qkv_weight.shape[1] // head_dim - query_heads) // 2
    group = query_heads // kv_heads
    ffn_units = down_weight.shape[1]
    rank = laurel_down.shape[1]
    score_scale = 1.0 / math.sqrt(head_dim)
    reps = 1 << len(rep_axes)
    line = 1 << len(line_axes)
    teams = 1 << len(far_axes)
    cores = 2
    core = lax.axis_index("core")
    rep = place_on(rep_axes)
    near = lax.axis_index(near_axis)
    weight_rows = qkv_weight.shape[0]
    group_width = group * head_dim
    kv_width = 2 * head_dim
    query_part = group_width // reps
    kv_part = kv_width // reps
    units = ffn_units // reps
    pair = 2 * tokens
    assert kv_heads == cores and pair >= WINDOW

    order = Order()
    go, mark, put, wait = order.go, order.mark, order.put, order.wait

    def waits(*transfers):
        wait(*[transfer for transfer in transfers if transfer is not None])

    def qkv_columns(c):
        key_start = query_heads * head_dim + c * head_dim
        value_start = (query_heads + kv_heads) * head_dim + c * head_dim
        offset = rep * kv_part
        kv_start = jnp.where(offset < head_dim, key_start + offset, value_start + offset - head_dim)
        return jnp.concatenate(
            [
                lax.dynamic_slice_in_dim(
                    qkv_weight, c * group_width + rep * query_part, query_part, 1
                ),
                lax.dynamic_slice_in_dim(qkv_weight, kv_start, kv_part, 1),
            ],
            axis=1,
        )

    def out_columns(c):
        return lax.dynamic_slice_in_dim(
            out_weight, c * group_width + rep * query_part, query_part, 1
        )

    ple = layer_gate.shape[1]
    ple_part = ple // reps
    attention_rows = jnp.concatenate(
        [qkv_columns(c) for c in range(cores)]
        + [out_columns(c) for c in range(cores)]
        + [
            laurel_down,
            laurel_up,
            lax.dynamic_slice_in_dim(layer_gate, rep * ple_part, ple_part, 1),
            lax.dynamic_slice_in_dim(layer_project, rep * ple_part, ple_part, 1),
        ],
        axis=1,
    )
    attention_whole = lax.all_gather(attention_rows, shard_axes, axis=0, tiled=True)
    part = query_part + kv_part
    qkv_own = lax.dynamic_slice_in_dim(attention_whole, core * part, part, 1)
    out_own = lax.dynamic_slice_in_dim(
        attention_whole, cores * part + core * query_part, query_part, 1
    )

    def ffn_rows(source, start):
        return lax.dynamic_slice_in_dim(source, start + rep * units, units, 1)

    ffn_mine = jnp.concatenate(
        [
            ffn_rows(gate_up_weight, 0),
            ffn_rows(gate_up_weight, ffn_units),
            ffn_rows(down_weight, 0),
        ],
        axis=1,
    )
    hidden_sent = put(hidden_in, "core")
    pos_sent = put(positions, "core")
    wait(hidden_sent, pos_sent)

    hidden_pair = jnp.concatenate([hidden_in, hidden_sent.value], axis=0)
    pos_pair = jnp.concatenate([positions, pos_sent.value], axis=0)
    steps = jnp.arange(tokens, dtype=jnp.int32)
    index = jnp.concatenate([core * tokens + steps, (1 - core) * tokens + steps])
    hidden_f = hidden_in.astype(F32)
    first_pair = scaled_norm(hidden_pair.astype(F32), model_gains[0]).astype(BF)
    normed_one, norm_one_pull = jax.vjp(scaled_norm, hidden_f, model_gains[0])
    cosine, sine_part = rope_tables(pos_pair, head_dim)
    first_pair, cosine, sine_part = mark(first_pair, cosine, sine_part)
    first_norm = first_pair[:tokens]
    ffn_mine, qkv_own, out_own = mark(*go(ffn_mine, qkv_own, out_own))
    ffn_whole = lax.all_gather(ffn_mine, shard_axes, axis=0, tiled=True)
    gate_up_cols = ffn_whole[:, : 2 * units]
    down_cols = ffn_whole[:, 2 * units :]
    qkv_gather = Gather(qkv_own, rep_axes, order)
    small_full = go(attention_whole)[0][:, cores * (part + query_part) :]
    down_low_full = small_full[:, :rank]
    up_low_full = small_full[:, rank : 2 * rank]
    ple_own = small_full[:, 2 * rank :]
    middle = dot_plain(first_norm, down_low_full).astype(BF)
    side_pre, middle = mark(dot_right_t(middle, up_low_full), middle)
    waits(*qkv_gather.sent)
    qkv_gather.next()
    waits(*qkv_gather.sent)
    ordered_heads = query_part != head_dim

    def head_order(blocks):
        return reorder(blocks, rep_axes) if ordered_heads else blocks

    out_gather = Gather(go(out_own)[0], rep_axes, order)
    qkv_blocks = qkv_gather.blocks()
    (qkv_part,) = mark(
        jnp.concatenate(
            head_order([block[:, :query_part] for block in qkv_blocks])
            + reorder([block[:, query_part:] for block in qkv_blocks], rep_axes),
            axis=1,
        )
    )
    proj = dot_plain(first_pair, qkv_part)
    query_pre = proj[:, :group_width].reshape(pair, group, head_dim)
    key_pre = proj[:, group_width : group_width + head_dim].reshape(pair, 1, head_dim)
    value_own = proj[:, group_width + head_dim :].astype(BF)

    def prepare(query_in, key_in, query_gain, key_gain):
        return (
            rotate(scaled_norm(query_in, query_gain), cosine, sine_part),
            rotate(scaled_norm(key_in, key_gain), cosine, sine_part),
        )

    (query_rot, key_rot), prepare_pull = jax.vjp(
        prepare, query_pre, key_pre, head_gains[0], head_gains[1]
    )
    query_low = query_rot.astype(BF)
    own_keys = jnp.concatenate([key_rot.astype(BF).reshape(pair, head_dim), value_own], axis=1)
    own_keys, query_low = mark(own_keys, query_low)
    keys_sent = Transfer(
        lax.ppermute(own_keys, line_axes, [(i, i + 1) for i in range(line - 1)])
    )
    waits(keys_sent, *out_gather.sent)
    out_gather.next()
    earlier = keys_sent.value
    all_keys = jnp.concatenate([earlier, own_keys], axis=0)
    key_all = all_keys[:, :head_dim]
    value_all = all_keys[:, head_dim:]
    key_index = jnp.concatenate([index - pair, index])
    offsets = index[:, None] - key_index[None, :]
    valid_keys = (offsets >= 0) & (offsets < WINDOW) & (offsets <= pos_pair[:, None])

    def masked_scores():
        raw = jnp.einsum("qgd,kd->gqk", query_low, key_all, preferred_element_type=F32)
        return jnp.where(valid_keys, raw * score_scale, -1e30)

    scores = masked_scores()
    row_max = jnp.max(scores, axis=-1, keepdims=True)
    exponents = jnp.exp(scores - row_max)
    row_total = jnp.sum(exponents, axis=-1, keepdims=True)
    log_total = row_max + jnp.log(row_total)
    probs_low = (exponents / row_total).astype(BF)
    mixed = jnp.einsum("gqk,kd->qgd", probs_low, value_all, preferred_element_type=F32)
    (mixed_low,) = mark(mixed.reshape(pair, group_width).astype(BF))
    waits(*out_gather.sent)
    (out_part,) = mark(jnp.concatenate(head_order(out_gather.blocks()), axis=1))
    (attn_sum,) = mark(dot_right_t(mixed_low, out_part))
    attn_sent = put(attn_sum[tokens:], "core")
    wait(attn_sent)
    attn_pre = attn_sum[:tokens] + attn_sent.value
    attn_out, attn_pull = jax.vjp(scaled_norm, attn_pre, model_gains[1])
    side_out, side_pull = jax.vjp(scaled_norm, side_pre, model_gains[2])
    first_sum = (hidden_f + attn_out + first_norm.astype(F32) + side_out) * SQRT_HALF
    normed_two, norm_two_pull = jax.vjp(scaled_norm, first_sum, model_gains[3])
    second_norm, first_sum = mark(normed_two.astype(BF), first_sum)

    team = reps
    staged = team == 4
    groups = [[0], [1, 2], [3]] if staged else [list(range(team))]

    def group_of(blocks, g):
        return jnp.concatenate([blocks[k] for k in groups[g]], axis=0)

    def by_block(results):
        parts = [None] * team
        for group, result in zip(groups, results):
            for i, k in enumerate(group):
                parts[k] = result[i * tokens : (i + 1) * tokens]
        return parts

    def step_blocks(gather, g):
        if not staged:
            return group_of(gather.blocks(), 0)
        if g == 0:
            return gather.value
        if g == 1:
            return jnp.concatenate(gather.near_blocks()[1:], axis=0)
        return gather.far_block()

    second_gather = Gather(second_norm, team_axes, order)
    waits(*second_gather.sent)
    second_gather.next()
    waits(*second_gather.sent)
    first_gather = Gather(go(first_norm)[0], rep_axes, order)
    ple_gather = Gather(go(ple_own)[0], rep_axes, order)
    waits(*first_gather.sent, *ple_gather.sent)
    first_gather.next()
    ple_gather.next()
    waits(*first_gather.sent, *ple_gather.sent)
    (second_all,) = mark(jnp.concatenate(go(*second_gather.blocks()), axis=0))
    gate_up = dot_plain(second_all, gate_up_cols)
    hidden_all = (gelu_tanh(gate_up[:, :units]) * gate_up[:, units:]).astype(BF)
    gate_up, hidden_all = mark(gate_up, hidden_all)
    (norm_all,) = mark(dot_right_t(hidden_all, down_cols).astype(BF))
    ffn_scatter = Scatter(
        [norm_all[k * tokens : (k + 1) * tokens] for k in range(team)], team_axes, order
    )
    ple_blocks = reorder(go(*ple_gather.blocks()), rep_axes)
    gate_layer_full, project_full = mark(
        jnp.concatenate([block[:, :ple_part] for block in ple_blocks], axis=1),
        jnp.concatenate([block[:, ple_part:] for block in ple_blocks], axis=1),
    )
    first_others = jnp.stack(go(*first_gather.blocks()[1:]))
    first_sent = put(first_others, "core")
    waits(*ffn_scatter.sent)
    ffn_scatter.next()
    (gate_up,) = go(gate_up)
    ffn_value, ffn_slope = mark(*gelu_terms(gate_up[:, :units], gate_up[:, units:]))
    wait(first_sent)
    (first_all,) = mark(
        jnp.concatenate(
            [first_pair]
            + [block for pair_blocks in zip(first_others, first_sent.value) for block in pair_blocks],
            axis=0,
        )
    )
    waits(*ffn_scatter.sent)
    (ffn_pre,) = mark(ffn_scatter.total())
    ffn_out, ffn_pull = jax.vjp(scaled_norm, ffn_pre, model_gains[4])
    second_sum = first_sum + ffn_out
    second_low = second_sum.astype(BF)
    ple_pre = dot_plain(second_low, gate_layer_full)

    def gate_vectors(pre_values, vector_values):
        return gelu_tanh(pre_values) * vector_values

    gated_val, gated_pull = jax.vjp(gate_vectors, ple_pre, layer_vectors.astype(F32))
    gated_low = gated_val.astype(BF)
    last_pre = dot_right_t(gated_low, project_full)
    last_out, last_pull = jax.vjp(scaled_norm, last_pre, model_gains[5])
    layer_out = (second_sum + last_out).astype(BF)

    upstream = cotangent.astype(F32)
    d_last, grad_gain_five = last_pull(upstream)
    d_last_low = d_last.astype(BF)
    d_gated = dot_plain(d_last_low, project_full)
    d_ple_pre, grad_vectors = gated_pull(d_gated)
    d_ple_low = d_ple_pre.astype(BF)
    d_second = upstream + dot_right_t(d_ple_low, gate_layer_full)
    d_ffn, grad_gain_four = ffn_pull(d_second)
    (d_ffn_low,) = mark(d_ffn.astype(BF))
    ple_terms = jnp.concatenate(
        [dot_left_t(second_low, d_ple_low), dot_left_t(d_last_low, gated_low)], axis=1
    ).astype(BF)
    ple_rows = lax.psum_scatter(ple_terms, shard_axes, scatter_dimension=0, tiled=True)
    d_ffn_gather = Gather(d_ffn_low, team_axes, order)
    d_ffn_groups, d_gate_groups, d_norm_groups = [], [], []

    def back_step(g):
        d_ffn_groups.append(step_blocks(d_ffn_gather, g))
        (block,) = go(d_ffn_groups[-1])
        at = sum(len(group) for group in groups[:g]) * tokens
        rows = slice(at, at + len(groups[g]) * tokens)
        value, slope = ffn_value[rows], ffn_slope[rows]
        d_hidden = dot_plain(block, down_cols)
        d_gate = (d_hidden * slope.astype(F32)).astype(BF)
        d_up = (d_hidden * value.astype(F32)).astype(BF)
        d_gate_groups.append(jnp.concatenate([d_gate, d_up], axis=1))
        d_norm = dot_right_t(d_gate_groups[-1], gate_up_cols).astype(BF)
        d_norm_groups.extend(mark(d_norm))

    if staged:
        waits(*d_ffn_gather.sent)
        d_ffn_gather.next()
        back_step(0)
        waits(*d_ffn_gather.sent)
    (d_ffn_all,) = mark(jnp.concatenate(go(*d_ffn_gather.blocks()), axis=0))
    (down_terms,) = mark(gradient_terms(d_ffn_all, hidden_all, units, 0))
    for g in range(1 if staged else 0, len(groups)):
        back_step(g)
    norm_scatter = Scatter(by_block(d_norm_groups), team_axes, order)

    def keep(value, axis, dim):
        return pick(value, lax.axis_index(axis), dim)

    def send(value, axis, dim):
        return put(pick(value, 1 - lax.axis_index(axis), dim), axis)

    def far_send(value):
        return send(value, far_axes[0], 0) if len(far_axes) == 1 else None

    def far_halve(value, transfer):
        if len(far_axes) == 1:
            return combine(keep(value, far_axes[0], 0), transfer.value)
        for axis in far_axes:
            value = value.reshape((2, value.shape[0] // 2) + value.shape[1:])
            value = combine(
                keep(value, axis, 0), swap(pick(value, 1 - lax.axis_index(axis), 0), axis)
            )
        return value

    class FfnGradient:
        def __init__(self, term):
            self.mine = lax.psum_scatter(term, shard_axes, scatter_dimension=0, tiled=True)

        def spread(self):
            self.gather = Gather(go(self.mine)[0], rep_axes, order)

        def place(self, whole, blocks, first, start=0):
            for k, block in enumerate(go(*blocks), first):
                whole = lax.dynamic_update_slice(
                    whole, block.astype(F32), (0, start + rep_of(k) * units)
                )
            return mark(whole)[0]

    def rep_of(k):
        return rep ^ k

    down_terms, ple_rows = lax.optimization_barrier((down_terms, ple_rows))
    down_grad = FfnGradient(down_terms)
    waits(*norm_scatter.sent)
    norm_scatter.next()
    (d_gate_all,) = mark(jnp.concatenate(go(*d_gate_groups), axis=0))
    (gate_terms,) = mark(gradient_terms(second_all, d_gate_all, units, 0))
    gate_grad = FfnGradient(gate_terms)
    (up_terms,) = mark(gradient_terms(go(second_all)[0], d_gate_all, units, 1))
    up_grad = FfnGradient(up_terms)
    waits(*norm_scatter.sent)
    d_second_norm = norm_scatter.total()
    d_first_part, grad_gain_three = norm_two_pull(d_second_norm)
    d_branch = (d_second + d_first_part) * SQRT_HALF
    d_attn, grad_gain_one = attn_pull(d_branch)
    d_attn_low, d_branch = mark(d_attn.astype(BF), d_branch)
    d_attn_sent = put(d_attn_low, "core")
    d_side, grad_gain_two = side_pull(go(d_branch)[0])
    d_side_low = d_side.astype(BF)
    d_middle_low = dot_plain(d_side_low, up_low_full).astype(BF)
    laurel_terms = jnp.concatenate(
        [dot_left_t(first_norm, d_middle_low), dot_left_t(d_side_low, middle)], axis=1
    ).astype(BF)
    d_middle_low, laurel_terms = mark(d_middle_low, laurel_terms)
    wait(d_attn_sent)
    d_attn_pair = jnp.concatenate([d_attn_low, d_attn_sent.value], axis=0)
    (d_mixed_low,) = mark(dot_plain(d_attn_pair, out_part).astype(BF))
    d_mixed_low = d_mixed_low.reshape(pair, group, head_dim)
    (out_term,) = mark(dot_left_t(go(d_attn_pair)[0], mixed_low).astype(BF))

    def columns(value):
        return jnp.split(value, reps, axis=1)

    out_scatter = Scatter(head_order(columns(go(out_term)[0])), rep_axes, order)
    probabilities = jnp.exp(masked_scores() - log_total)
    (d_mixed_low,) = go(d_mixed_low)
    d_probs = jnp.einsum("qgd,kd->gqk", d_mixed_low, value_all, preferred_element_type=F32)
    row_dot = jnp.sum(probabilities * d_probs, axis=-1, keepdims=True)
    (d_scores,) = mark((probabilities * (d_probs - row_dot)).astype(BF))
    small_sum = go(ple_rows)[0]
    small_sent = put(small_sum, rep_axes[0])
    waits(small_sent, *out_scatter.sent)
    out_scatter.next()
    for axis in rep_axes[1:]:
        small_sum = combine(small_sum, small_sent.value)
        small_sent = put(small_sum, axis)
    (d_scores,) = go(d_scores)
    d_values = jnp.einsum("gqk,qgd->kd", probs_low, d_mixed_low, preferred_element_type=F32)
    d_keys = (
        jnp.einsum("gqk,qgd->kd", d_scores, query_low, preferred_element_type=F32) * score_scale
    )
    (key_grads,) = mark(jnp.concatenate([d_keys, d_values], axis=1))
    returned = Transfer(
        lax.ppermute(
            key_grads[:pair].astype(BF), line_axes, [(i + 1, i) for i in range(line - 1)]
        )
    )
    d_queries = (
        jnp.einsum("gqk,kd->qgd", go(d_scores)[0], key_all, preferred_element_type=F32)
        * score_scale
    )
    (d_queries,) = mark(d_queries)
    down_grad.spread()
    waits(returned, small_sent, *out_scatter.sent, *down_grad.gather.sent)
    ple_sum = small_sum.astype(F32) + small_sent.value.astype(F32)
    own_grads = key_grads[pair:] + returned.value.astype(F32)
    d_query_pre, d_key_pre, grad_query_gain, grad_key_gain = prepare_pull(
        (d_queries, own_grads[:, :head_dim].reshape(pair, 1, head_dim))
    )
    d_proj = jnp.concatenate(
        [
            d_query_pre.reshape(pair, group_width),
            d_key_pre.reshape(pair, head_dim),
            own_grads[:, head_dim:],
        ],
        axis=1,
    ).astype(BF)
    (d_proj,) = mark(d_proj)

    def rep_put(value, k):
        return Transfer(lax.ppermute(value, rep_axes, [(i, i ^ k) for i in range(reps)]))

    proj_parts = [
        jnp.concatenate([one, two], axis=1)
        for one, two in zip(
            head_order(columns(d_proj[:, :group_width])),
            reorder(columns(d_proj[:, group_width:]), rep_axes),
        )
    ]
    proj_sent = [rep_put(proj_parts[k], k) for k in range(1, reps)]
    down_grad.gather.next()
    (out_total,) = mark(out_scatter.total().astype(BF))
    waits(*proj_sent, *down_grad.gather.sent)
    proj_all = jnp.concatenate([proj_parts[0]] + [part.value for part in proj_sent], axis=0)
    (qkv_total,) = mark(dot_left_t(first_all, go(proj_all)[0]).astype(BF))

    def core_columns(value):
        return [jnp.where(core == c, value, jnp.zeros_like(value)) for c in range(cores)]

    (attention_terms,) = mark(
        jnp.concatenate(
            core_columns(qkv_total) + core_columns(out_total) + [laurel_terms], axis=1
        )
    )
    attention_sum = lax.psum_scatter(
        attention_terms, shard_axes, scatter_dimension=0, tiled=True
    )
    gate_grad.spread()
    (norm_sum,) = mark(dot_right_t(go(d_proj)[0], qkv_part))
    norm_sent = put(norm_sum[tokens:], "core")
    waits(norm_sent, *gate_grad.gather.sent)
    gate_grad.gather.next()
    d_first_norm = (
        norm_sum[:tokens]
        + norm_sent.value
        + dot_right_t(d_middle_low, down_low_full)
        + d_branch
    )
    d_input_part, grad_gain_zero = norm_one_pull(d_first_norm)
    grad_hidden, grad_gain_zero = mark(d_branch + d_input_part, grad_gain_zero)
    model_part = jnp.stack(
        [
            grad_gain_zero,
            grad_gain_one,
            grad_gain_two,
            grad_gain_three,
            grad_gain_four,
            grad_gain_five,
        ]
    )
    head_part = jnp.stack([grad_query_gain, grad_key_gain])
    gains = jnp.concatenate([model_part.reshape(-1, head_dim), head_part], axis=0)
    gain_axes = rep_axes + line_axes + ("core",)

    def gain_put(pair_axes):
        if len(pair_axes) == 1:
            return [put(gains, pair_axes[0])]
        across = lax.ppermute(gains, pair_axes, [(i, 3 - i) for i in range(4)])
        return [put(gains, pair_axes[0]), put(gains, pair_axes[1]), Transfer(across)]

    def gain_sum(transfers):
        values = [transfer.value for transfer in transfers]
        if len(values) == 1:
            return gains + values[0]
        return (gains + values[0]) + (values[1] + values[2])

    gain_steps = [gain_axes[i : i + 2] for i in range(0, len(gain_axes), 2)]
    gain_sent = gain_put(gain_steps[0])
    grad_down = jnp.zeros((weight_rows, ffn_units), F32)
    grad_down = down_grad.place(grad_down, down_grad.gather.blocks(), 0)
    waits(*gain_sent, *gate_grad.gather.sent)
    up_grad.spread()
    gains = gain_sum(gain_sent)
    for step in gain_steps[1:-2]:
        gain_sent = gain_put(step)
        waits(*gain_sent)
        gains = gain_sum(gain_sent)
    gain_sent = gain_put(gain_steps[-2])
    grad_gate_up = jnp.zeros((weight_rows, 2 * ffn_units), F32)
    grad_gate_up = gate_grad.place(grad_gate_up, gate_grad.gather.blocks(), 0)
    waits(*gain_sent, *up_grad.gather.sent)
    up_grad.gather.next()
    gains = gain_sum(gain_sent)
    gain_sent = gain_put(gain_steps[-1])
    if staged:
        grad_gate_up = up_grad.place(grad_gate_up, up_grad.gather.near_blocks(), 0, ffn_units)
    waits(*gain_sent, *up_grad.gather.sent)
    gains = gain_sum(gain_sent)
    if staged:
        far_block = [up_grad.gather.far_block()]
        grad_gate_up = up_grad.place(grad_gate_up, far_block, 3, ffn_units)
    else:
        grad_gate_up = up_grad.place(grad_gate_up, up_grad.gather.blocks(), 0, ffn_units)
    (attention_sum,) = go(attention_sum)
    attention_width = cores * (part + query_part)
    attention_gather = Gather(attention_sum[:, :attention_width], rep_axes, order)
    laurel_sum = attention_sum[:, attention_width:]
    laurel_sent = put(laurel_sum, rep_axes[0])
    waits(laurel_sent, *attention_gather.sent)
    attention_gather.next()
    for axis in rep_axes[1:]:
        laurel_sum = combine(laurel_sum, laurel_sent.value)
        laurel_sent = put(laurel_sum, axis)
    waits(laurel_sent, *attention_gather.sent)
    attention_blocks = reorder(attention_gather.blocks(), rep_axes)
    grad_qkv = jnp.concatenate(
        [
            block[:, c * part : c * part + query_part].astype(F32)
            for c in range(cores)
            for block in attention_blocks
        ]
        + [
            block[:, c * part + query_part : (c + 1) * part].astype(F32)
            for half in (attention_blocks[: reps // 2], attention_blocks[reps // 2 :])
            for c in range(cores)
            for block in half
        ],
        axis=1,
    )
    grad_out = jnp.concatenate(
        [
            block[:, cores * part + c * query_part : cores * part + (c + 1) * query_part].astype(
                F32
            )
            for c in range(cores)
            for block in attention_blocks
        ],
        axis=1,
    )
    laurel_sum = laurel_sum.astype(F32) + laurel_sent.value.astype(F32)
    grad_laurel_down, grad_laurel_up = laurel_sum[:, :rank], laurel_sum[:, rank:]
    grad_layer_gate, grad_layer_project = ple_sum[:, :ple], ple_sum[:, ple:]
    grad_model_gains = gains[: -head_part.shape[0]].reshape(model_part.shape)
    grad_head_gains = gains[-head_part.shape[0] :]
    return (
        layer_out,
        grad_hidden,
        grad_vectors,
        grad_model_gains,
        grad_head_gains,
        grad_qkv,
        grad_out,
        grad_laurel_down,
        grad_laurel_up,
        grad_gate_up,
        grad_down,
        grad_layer_gate,
        grad_layer_project,
    )


def solution(mesh):
    reps, shards = mesh.shape["rep"], mesh.shape["shard"]
    rep_axes = tuple(f"rep{i}" for i in range(reps.bit_length() - 1))
    line_axes = tuple(f"line{i}" for i in range(shards.bit_length() - 2))
    axes = rep_axes + line_axes + ("core",)
    assert 1 << len(axes) == reps * shards
    fine = Mesh(np.asarray(mesh.devices).reshape((2,) * len(axes)), axes)
    rows, owned = P(axes, None), P(line_axes + ("core",), None)
    return jax.shard_map(
        functools.partial(body, rep_axes, line_axes),
        mesh=fine,
        in_specs=(rows, rows, P(axes), rows, P(), P()) + (owned,) * 8,
        out_specs=(rows, rows, rows, P(), P()) + (owned,) * 8,
        check_vma=False,
    )
```

```python
import functools
import math

import jax
import jax.numpy as jnp
import numpy as np
from jax import lax
from jax.experimental import pallas as pl
from jax.experimental.pallas import tpu as pltpu
from jax.sharding import Mesh
from jax.sharding import PartitionSpec as P

WINDOW = 512
EPSILON = 1e-06
SQRT_HALF = 0.7071067811865476
BF = jnp.bfloat16
F32 = jnp.float32


def scaled_norm(values, gain_row):
    return (
        values * lax.rsqrt(jnp.mean(values * values, axis=-1, keepdims=True) + EPSILON) * gain_row
    )


def rotate(values, cosine, sine_part):
    half_dim = values.shape[-1] // 2
    first_half = values[..., :half_dim]
    second_half = values[..., half_dim:]
    return jnp.concatenate(
        [
            first_half * cosine - second_half * sine_part,
            second_half * cosine + first_half * sine_part,
        ],
        axis=-1,
    )


def rope_tables(positions, head_dim):
    half_dim = head_dim // 2
    frequency = jnp.exp(
        jnp.arange(half_dim, dtype=jnp.float32) * (-2.0 * math.log(10000.0) / head_dim)
    )
    phase_angle = positions.astype(jnp.float32)[:, None] * frequency[None, :]
    return (jnp.cos(phase_angle)[:, None, :], jnp.sin(phase_angle)[:, None, :])


def dot_plain(left_side, right_side):
    return jnp.dot(left_side, right_side, preferred_element_type=jnp.float32)


def dot_right_t(left_side, right_side):
    return lax.dot_general(
        left_side, right_side, (((1,), (1,)), ((), ())), preferred_element_type=jnp.float32
    )


def dot_left_t(left_side, right_side):
    return lax.dot_general(
        left_side, right_side, (((0,), (0,)), ((), ())), preferred_element_type=jnp.float32
    )


def terms_kernel(left_ref, right_ref, out_ref):
    out_ref[...] = dot_left_t(left_ref[...], right_ref[...]).astype(out_ref.dtype)


def gradient_terms(left_side, right_side, size, block):
    rows, columns = left_side.shape
    step = math.gcd(columns, 512)
    return pl.pallas_call(
        terms_kernel,
        grid=(columns // step,),
        in_specs=[
            pl.BlockSpec((rows, step), lambda i: (0, i)),
            pl.BlockSpec((rows, size), lambda i: (0, block)),
        ],
        out_specs=pl.BlockSpec((step, size), lambda i: (i, 0)),
        out_shape=jax.ShapeDtypeStruct((columns, size), BF),
        cost_estimate=pl.CostEstimate(flops=1, bytes_accessed=1, transcendentals=0),
        compiler_params=pltpu.CompilerParams(vmem_limit_bytes=40 * 1024 * 1024),
    )(left_side, right_side)


def gelu_tanh(values):
    return jax.nn.gelu(values, approximate=True)


def after(value, *others):
    return lax.optimization_barrier((value,) + others)[0]


def gelu_terms(gate, up):
    root = 0.7978845608
    square = gate * gate
    bend = jnp.tanh(root * (gate + 0.044715 * gate * square))
    half = 0.5 * (1.0 + bend)
    value = gate * half
    slope = half + 0.5 * gate * (1.0 - bend * bend) * root * (1.0 + 3.0 * 0.044715 * square)
    return value.astype(BF), (slope * up).astype(BF)


def swap(value, axis):
    return lax.ppermute(value, axis, [(0, 1), (1, 0)])


def place_on(axes):
    place = jnp.int32(0)
    for axis in axes:
        place = place * 2 + lax.axis_index(axis)
    return place


def combine(*values):
    total = values[0].astype(F32)
    for value in values[1:]:
        total = total + value.astype(F32)
    return total.astype(BF)


class Order:
    def __init__(self):
        self.last = ()

    def go(self, *values):
        return list(lax.optimization_barrier(values + self.last)[: len(values)])

    def mark(self, *values):
        self.last = tuple(values)
        return list(values)

    def put(self, value, axis):
        return Transfer(swap(value, axis))

    def wait(self, *transfers):
        for transfer, value in zip(
            transfers, self.mark(*self.go(*[transfer.value for transfer in transfers]))
        ):
            transfer.value = value


class Transfer:
    def __init__(self, value):
        self.value = value


class Gather:
    def __init__(self, value, axes, order):
        self.axes, self.order, self.value = axes, order, value
        self.sent = [order.put(value, axis) for axis in axes] if len(axes) == 2 else []
        self.first = self.sent

    def next(self):
        if len(self.axes) == 2:
            half = self.value.shape[0] // 2
            from_one, from_two = [transfer.value for transfer in self.sent]
            self.sent = [
                self.order.put(from_two[half:], self.axes[0]),
                self.order.put(from_one[:half], self.axes[1]),
            ]

    def near_blocks(self):
        return [self.value, self.first[1].value, self.first[0].value]

    def far_block(self):
        return jnp.concatenate([self.sent[1].value, self.sent[0].value], axis=0)

    def blocks(self):
        if len(self.axes) == 2:
            return self.near_blocks() + [self.far_block()]
        blocks = [self.value]
        for axis in reversed(self.axes):
            blocks = blocks + [swap(block, axis) for block in blocks]
        return blocks


class Scatter:
    def __init__(self, parts, axes, order):
        self.parts, self.axes, self.order = parts, axes, order
        self.half = parts[0].shape[0] // 2
        self.sent = []
        if len(axes) == 2:
            self.sent = [
                order.put(parts[3][self.half :], axes[0]),
                order.put(parts[3][: self.half], axes[1]),
            ]

    def next(self):
        if len(self.axes) == 2:
            half, (own, one, two, far) = self.half, self.parts
            via_two, via_one = [transfer.value for transfer in self.sent]
            two = jnp.concatenate([combine(two[:half], via_one), two[half:]], axis=0)
            one = jnp.concatenate([one[:half], combine(one[half:], via_two)], axis=0)
            self.sent = [self.order.put(two, self.axes[0]), self.order.put(one, self.axes[1])]

    def total(self):
        parts = self.parts
        if len(self.axes) != 2:
            for axis in self.axes:
                half = len(parts) // 2
                parts = [
                    combine(mine, swap(theirs, axis))
                    for mine, theirs in zip(parts[:half], parts[half:])
                ]
            return parts[0].astype(F32)
        total = parts[0].astype(F32)
        for transfer in self.sent:
            total = total + transfer.value.astype(F32)
        return total


def reorder(blocks, axes):
    count = len(axes)
    for bit, axis in enumerate(reversed(axes)):
        flip = lax.axis_index(axis) == 1
        blocks = [jnp.where(flip, blocks[k ^ (1 << bit)], blocks[k]) for k in range(1 << count)]
    return blocks


def stack_pair(mine, other, axis, dim):
    first = lax.axis_index(axis) == 0
    return jnp.stack([jnp.where(first, mine, other), jnp.where(first, other, mine)], axis=dim)


def pick(value, which, dim=0):
    return lax.dynamic_index_in_dim(value, which, dim, keepdims=False)


def body(
    rep_axes,
    line_axes,
    hidden_in,
    layer_vectors,
    positions,
    cotangent,
    model_gains,
    head_gains,
    qkv_weight,
    out_weight,
    laurel_down,
    laurel_up,
    gate_up_weight,
    down_weight,
    layer_gate,
    layer_project,
):
    far_axes, near_axis = line_axes[:-1], line_axes[-1]
    team_axes = rep_axes
    shard_axes = line_axes + ("core",)
    tokens, width = hidden_in.shape
    head_dim = head_gains.shape[1]
    query_heads = out_weight.shape[1] // head_dim
    kv_heads = (qkv_weight.shape[1] // head_dim - query_heads) // 2
    group = query_heads // kv_heads
    ffn_units = down_weight.shape[1]
    rank = laurel_down.shape[1]
    score_scale = 1.0 / math.sqrt(head_dim)
    reps = 1 << len(rep_axes)
    line = 1 << len(line_axes)
    teams = 1 << len(far_axes)
    cores = 2
    core = lax.axis_index("core")
    rep = place_on(rep_axes)
    near = lax.axis_index(near_axis)
    weight_rows = qkv_weight.shape[0]
    group_width = group * head_dim
    kv_width = 2 * head_dim
    query_part = group_width // reps
    kv_part = kv_width // reps
    units = ffn_units // reps
    pair = 2 * tokens
    assert kv_heads == cores and pair >= WINDOW

    order = Order()
    go, mark, put, wait = order.go, order.mark, order.put, order.wait

    def waits(*transfers):
        wait(*[transfer for transfer in transfers if transfer is not None])

    def qkv_columns(c):
        key_start = query_heads * head_dim + c * head_dim
        value_start = (query_heads + kv_heads) * head_dim + c * head_dim
        offset = rep * kv_part
        kv_start = jnp.where(offset < head_dim, key_start + offset, value_start + offset - head_dim)
        return jnp.concatenate(
            [
                lax.dynamic_slice_in_dim(
                    qkv_weight, c * group_width + rep * query_part, query_part, 1
                ),
                lax.dynamic_slice_in_dim(qkv_weight, kv_start, kv_part, 1),
            ],
            axis=1,
        )

    def out_columns(c):
        return lax.dynamic_slice_in_dim(
            out_weight, c * group_width + rep * query_part, query_part, 1
        )

    ple = layer_gate.shape[1]
    ple_part = ple // reps
    attention_rows = jnp.concatenate(
        [qkv_columns(c) for c in range(cores)]
        + [out_columns(c) for c in range(cores)]
        + [
            laurel_down,
            laurel_up,
            lax.dynamic_slice_in_dim(layer_gate, rep * ple_part, ple_part, 1),
            lax.dynamic_slice_in_dim(layer_project, rep * ple_part, ple_part, 1),
        ],
        axis=1,
    )
    attention_whole = lax.all_gather(attention_rows, shard_axes, axis=0, tiled=True)
    part = query_part + kv_part
    qkv_own = lax.dynamic_slice_in_dim(attention_whole, core * part, part, 1)
    out_own = lax.dynamic_slice_in_dim(
        attention_whole, cores * part + core * query_part, query_part, 1
    )

    def ffn_rows(source, start):
        return lax.dynamic_slice_in_dim(source, start + rep * units, units, 1)

    ffn_mine = jnp.concatenate(
        [
            ffn_rows(gate_up_weight, 0),
            ffn_rows(gate_up_weight, ffn_units),
            ffn_rows(down_weight, 0),
        ],
        axis=1,
    )
    hidden_sent = put(hidden_in, "core")
    pos_sent = put(positions, "core")
    wait(hidden_sent, pos_sent)

    hidden_pair = jnp.concatenate([hidden_in, hidden_sent.value], axis=0)
    pos_pair = jnp.concatenate([positions, pos_sent.value], axis=0)
    steps = jnp.arange(tokens, dtype=jnp.int32)
    index = jnp.concatenate([core * tokens + steps, (1 - core) * tokens + steps])
    hidden_f = hidden_in.astype(F32)
    first_pair = scaled_norm(hidden_pair.astype(F32), model_gains[0]).astype(BF)
    normed_one, norm_one_pull = jax.vjp(scaled_norm, hidden_f, model_gains[0])
    cosine, sine_part = rope_tables(pos_pair, head_dim)
    first_pair, cosine, sine_part = mark(first_pair, cosine, sine_part)
    first_norm = first_pair[:tokens]
    ffn_mine, qkv_own, out_own = mark(*go(ffn_mine, qkv_own, out_own))
    ffn_whole = lax.all_gather(ffn_mine, shard_axes, axis=0, tiled=True)
    gate_up_cols = ffn_whole[:, : 2 * units]
    down_cols = ffn_whole[:, 2 * units :]
    qkv_gather = Gather(qkv_own, rep_axes, order)
    small_full = go(attention_whole)[0][:, cores * (part + query_part) :]
    down_low_full = small_full[:, :rank]
    up_low_full = small_full[:, rank : 2 * rank]
    ple_own = small_full[:, 2 * rank :]
    middle = dot_plain(first_norm, down_low_full).astype(BF)
    side_pre, middle = mark(dot_right_t(middle, up_low_full), middle)
    waits(*qkv_gather.sent)
    qkv_gather.next()
    waits(*qkv_gather.sent)
    ordered_heads = query_part != head_dim

    def head_order(blocks):
        return reorder(blocks, rep_axes) if ordered_heads else blocks

    out_gather = Gather(go(out_own)[0], rep_axes, order)
    qkv_blocks = qkv_gather.blocks()
    (qkv_part,) = mark(
        jnp.concatenate(
            head_order([block[:, :query_part] for block in qkv_blocks])
            + reorder([block[:, query_part:] for block in qkv_blocks], rep_axes),
            axis=1,
        )
    )
    proj = dot_plain(first_pair, qkv_part)
    query_pre = proj[:, :group_width].reshape(pair, group, head_dim)
    key_pre = proj[:, group_width : group_width + head_dim].reshape(pair, 1, head_dim)
    value_own = proj[:, group_width + head_dim :].astype(BF)

    def prepare(query_in, key_in, query_gain, key_gain):
        return (
            rotate(scaled_norm(query_in, query_gain), cosine, sine_part),
            rotate(scaled_norm(key_in, key_gain), cosine, sine_part),
        )

    (query_rot, key_rot), prepare_pull = jax.vjp(
        prepare, query_pre, key_pre, head_gains[0], head_gains[1]
    )
    query_low = query_rot.astype(BF)
    own_keys = jnp.concatenate([key_rot.astype(BF).reshape(pair, head_dim), value_own], axis=1)
    own_keys, query_low = mark(own_keys, query_low)
    keys_sent = Transfer(
        lax.ppermute(own_keys, line_axes, [(i, i + 1) for i in range(line - 1)])
    )
    waits(keys_sent, *out_gather.sent)
    out_gather.next()
    earlier = keys_sent.value
    all_keys = jnp.concatenate([earlier, own_keys], axis=0)
    key_all = all_keys[:, :head_dim]
    value_all = all_keys[:, head_dim:]
    key_index = jnp.concatenate([index - pair, index])
    offsets = index[:, None] - key_index[None, :]
    valid_keys = (offsets >= 0) & (offsets < WINDOW) & (offsets <= pos_pair[:, None])

    def masked_scores():
        raw = jnp.einsum("qgd,kd->gqk", query_low, key_all, preferred_element_type=F32)
        return jnp.where(valid_keys, raw * score_scale, -1e30)

    scores = masked_scores()
    row_max = jnp.max(scores, axis=-1, keepdims=True)
    exponents = jnp.exp(scores - row_max)
    row_total = jnp.sum(exponents, axis=-1, keepdims=True)
    log_total = row_max + jnp.log(row_total)
    probs_low = (exponents / row_total).astype(BF)
    mixed = jnp.einsum("gqk,kd->qgd", probs_low, value_all, preferred_element_type=F32)
    (mixed_low,) = mark(mixed.reshape(pair, group_width).astype(BF))
    waits(*out_gather.sent)
    (out_part,) = mark(jnp.concatenate(head_order(out_gather.blocks()), axis=1))
    (attn_sum,) = mark(dot_right_t(mixed_low, out_part))
    attn_sent = put(attn_sum[tokens:], "core")
    wait(attn_sent)
    attn_pre = attn_sum[:tokens] + attn_sent.value
    attn_out, attn_pull = jax.vjp(scaled_norm, attn_pre, model_gains[1])
    side_out, side_pull = jax.vjp(scaled_norm, side_pre, model_gains[2])
    first_sum = (hidden_f + attn_out + first_norm.astype(F32) + side_out) * SQRT_HALF
    normed_two, norm_two_pull = jax.vjp(scaled_norm, first_sum, model_gains[3])
    second_norm, first_sum = mark(normed_two.astype(BF), first_sum)

    team = reps
    staged = team == 4
    groups = [[0], [1, 2], [3]] if staged else [list(range(team))]

    def group_of(blocks, g):
        return jnp.concatenate([blocks[k] for k in groups[g]], axis=0)

    def by_block(results):
        parts = [None] * team
        for group, result in zip(groups, results):
            for i, k in enumerate(group):
                parts[k] = result[i * tokens : (i + 1) * tokens]
        return parts

    def step_blocks(gather, g):
        if not staged:
            return group_of(gather.blocks(), 0)
        if g == 0:
            return gather.value
        if g == 1:
            return jnp.concatenate(gather.near_blocks()[1:], axis=0)
        return gather.far_block()

    second_gather = Gather(second_norm, team_axes, order)
    waits(*second_gather.sent)
    second_gather.next()
    waits(*second_gather.sent)
    first_gather = Gather(go(first_norm)[0], rep_axes, order)
    ple_gather = Gather(go(ple_own)[0], rep_axes, order)
    waits(*first_gather.sent, *ple_gather.sent)
    first_gather.next()
    ple_gather.next()
    waits(*first_gather.sent, *ple_gather.sent)
    (second_all,) = mark(jnp.concatenate(go(*second_gather.blocks()), axis=0))
    gate_up = dot_plain(second_all, gate_up_cols)
    hidden_all = (gelu_tanh(gate_up[:, :units]) * gate_up[:, units:]).astype(BF)
    gate_up, hidden_all = mark(gate_up, hidden_all)
    (norm_all,) = mark(dot_right_t(hidden_all, down_cols).astype(BF))
    ffn_scatter = Scatter(
        [norm_all[k * tokens : (k + 1) * tokens] for k in range(team)], team_axes, order
    )
    ple_blocks = reorder(go(*ple_gather.blocks()), rep_axes)
    gate_layer_full, project_full = mark(
        jnp.concatenate([block[:, :ple_part] for block in ple_blocks], axis=1),
        jnp.concatenate([block[:, ple_part:] for block in ple_blocks], axis=1),
    )
    first_others = jnp.stack(go(*first_gather.blocks()[1:]))
    first_sent = put(first_others, "core")
    waits(*ffn_scatter.sent)
    ffn_scatter.next()
    (gate_up,) = go(gate_up)
    ffn_value, ffn_slope = mark(*gelu_terms(gate_up[:, :units], gate_up[:, units:]))
    wait(first_sent)
    (first_all,) = mark(
        jnp.concatenate(
            [first_pair]
            + [block for pair_blocks in zip(first_others, first_sent.value) for block in pair_blocks],
            axis=0,
        )
    )
    waits(*ffn_scatter.sent)
    (ffn_pre,) = mark(ffn_scatter.total())
    ffn_out, ffn_pull = jax.vjp(scaled_norm, ffn_pre, model_gains[4])
    second_sum = first_sum + ffn_out
    second_low = second_sum.astype(BF)
    ple_pre = dot_plain(second_low, gate_layer_full)

    def gate_vectors(pre_values, vector_values):
        return gelu_tanh(pre_values) * vector_values

    gated_val, gated_pull = jax.vjp(gate_vectors, ple_pre, layer_vectors.astype(F32))
    gated_low = gated_val.astype(BF)
    last_pre = dot_right_t(gated_low, project_full)
    last_out, last_pull = jax.vjp(scaled_norm, last_pre, model_gains[5])
    layer_out = (second_sum + last_out).astype(BF)

    upstream = cotangent.astype(F32)
    d_last, grad_gain_five = last_pull(upstream)
    d_last_low = d_last.astype(BF)
    d_gated = dot_plain(d_last_low, project_full)
    d_ple_pre, grad_vectors = gated_pull(d_gated)
    d_ple_low = d_ple_pre.astype(BF)
    d_second = upstream + dot_right_t(d_ple_low, gate_layer_full)
    d_ffn, grad_gain_four = ffn_pull(d_second)
    (d_ffn_low,) = mark(d_ffn.astype(BF))
    ple_terms = jnp.concatenate(
        [dot_left_t(second_low, d_ple_low), dot_left_t(d_last_low, gated_low)], axis=1
    ).astype(BF)
    ple_rows = lax.psum_scatter(ple_terms, shard_axes, scatter_dimension=0, tiled=True)
    d_ffn_gather = Gather(d_ffn_low, team_axes, order)
    d_ffn_groups, d_gate_groups, d_norm_groups = [], [], []

    def back_step(g):
        d_ffn_groups.append(step_blocks(d_ffn_gather, g))
        (block,) = go(d_ffn_groups[-1])
        at = sum(len(group) for group in groups[:g]) * tokens
        rows = slice(at, at + len(groups[g]) * tokens)
        value, slope = ffn_value[rows], ffn_slope[rows]
        d_hidden = dot_plain(block, down_cols)
        d_gate = (d_hidden * slope.astype(F32)).astype(BF)
        d_up = (d_hidden * value.astype(F32)).astype(BF)
        d_gate_groups.append(jnp.concatenate([d_gate, d_up], axis=1))
        d_norm = dot_right_t(d_gate_groups[-1], gate_up_cols).astype(BF)
        d_norm_groups.extend(mark(d_norm))

    if staged:
        waits(*d_ffn_gather.sent)
        d_ffn_gather.next()
        back_step(0)
        waits(*d_ffn_gather.sent)
    (d_ffn_all,) = mark(jnp.concatenate(go(*d_ffn_gather.blocks()), axis=0))
    (down_terms,) = mark(gradient_terms(d_ffn_all, hidden_all, units, 0))
    for g in range(1 if staged else 0, len(groups)):
        back_step(g)
    norm_scatter = Scatter(by_block(d_norm_groups), team_axes, order)

    def keep(value, axis, dim):
        return pick(value, lax.axis_index(axis), dim)

    def send(value, axis, dim):
        return put(pick(value, 1 - lax.axis_index(axis), dim), axis)

    def far_send(value):
        return send(value, far_axes[0], 0) if len(far_axes) == 1 else None

    def far_halve(value, transfer):
        if len(far_axes) == 1:
            return combine(keep(value, far_axes[0], 0), transfer.value)
        for axis in far_axes:
            value = value.reshape((2, value.shape[0] // 2) + value.shape[1:])
            value = combine(
                keep(value, axis, 0), swap(pick(value, 1 - lax.axis_index(axis), 0), axis)
            )
        return value

    class FfnGradient:
        def __init__(self, term):
            self.mine = lax.psum_scatter(term, shard_axes, scatter_dimension=0, tiled=True)

        def spread(self):
            self.gather = Gather(go(self.mine)[0], rep_axes, order)

        def place(self, whole, blocks, first, start=0):
            for k, block in enumerate(go(*blocks), first):
                whole = lax.dynamic_update_slice(
                    whole, block.astype(F32), (0, start + rep_of(k) * units)
                )
            return mark(whole)[0]

    def rep_of(k):
        return rep ^ k

    down_terms, ple_rows = lax.optimization_barrier((down_terms, ple_rows))
    down_grad = FfnGradient(down_terms)
    waits(*norm_scatter.sent)
    norm_scatter.next()
    (d_gate_all,) = mark(jnp.concatenate(go(*d_gate_groups), axis=0))
    (gate_terms,) = mark(gradient_terms(second_all, d_gate_all, units, 0))
    gate_grad = FfnGradient(gate_terms)
    (up_terms,) = mark(gradient_terms(go(second_all)[0], d_gate_all, units, 1))
    up_grad = FfnGradient(up_terms)
    waits(*norm_scatter.sent)
    d_second_norm = norm_scatter.total()
    d_first_part, grad_gain_three = norm_two_pull(d_second_norm)
    d_branch = (d_second + d_first_part) * SQRT_HALF
    d_attn, grad_gain_one = attn_pull(d_branch)
    d_attn_low, d_branch = mark(d_attn.astype(BF), d_branch)
    d_attn_sent = put(d_attn_low, "core")
    d_side, grad_gain_two = side_pull(go(d_branch)[0])
    d_side_low = d_side.astype(BF)
    d_middle_low = dot_plain(d_side_low, up_low_full).astype(BF)
    laurel_terms = jnp.concatenate(
        [dot_left_t(first_norm, d_middle_low), dot_left_t(d_side_low, middle)], axis=1
    ).astype(BF)
    d_middle_low, laurel_terms = mark(d_middle_low, laurel_terms)
    wait(d_attn_sent)
    d_attn_pair = jnp.concatenate([d_attn_low, d_attn_sent.value], axis=0)
    (d_mixed_low,) = mark(dot_plain(d_attn_pair, out_part).astype(BF))
    d_mixed_low = d_mixed_low.reshape(pair, group, head_dim)
    (out_term,) = mark(dot_left_t(go(d_attn_pair)[0], mixed_low).astype(BF))

    def columns(value):
        return jnp.split(value, reps, axis=1)

    out_scatter = Scatter(head_order(columns(go(out_term)[0])), rep_axes, order)
    probabilities = jnp.exp(masked_scores() - log_total)
    (d_mixed_low,) = go(d_mixed_low)
    d_probs = jnp.einsum("qgd,kd->gqk", d_mixed_low, value_all, preferred_element_type=F32)
    row_dot = jnp.sum(probabilities * d_probs, axis=-1, keepdims=True)
    (d_scores,) = mark((probabilities * (d_probs - row_dot)).astype(BF))
    small_sum = go(ple_rows)[0]
    small_sent = put(small_sum, rep_axes[0])
    waits(small_sent, *out_scatter.sent)
    out_scatter.next()
    for axis in rep_axes[1:]:
        small_sum = combine(small_sum, small_sent.value)
        small_sent = put(small_sum, axis)
    (d_scores,) = go(d_scores)
    d_values = jnp.einsum("gqk,qgd->kd", probs_low, d_mixed_low, preferred_element_type=F32)
    d_keys = (
        jnp.einsum("gqk,qgd->kd", d_scores, query_low, preferred_element_type=F32) * score_scale
    )
    (key_grads,) = mark(jnp.concatenate([d_keys, d_values], axis=1))
    returned = Transfer(
        lax.ppermute(
            key_grads[:pair].astype(BF), line_axes, [(i + 1, i) for i in range(line - 1)]
        )
    )
    d_queries = (
        jnp.einsum("gqk,kd->qgd", go(d_scores)[0], key_all, preferred_element_type=F32)
        * score_scale
    )
    (d_queries,) = mark(d_queries)
    down_grad.spread()
    waits(returned, small_sent, *out_scatter.sent, *down_grad.gather.sent)
    ple_sum = small_sum.astype(F32) + small_sent.value.astype(F32)
    own_grads = key_grads[pair:] + returned.value.astype(F32)
    d_query_pre, d_key_pre, grad_query_gain, grad_key_gain = prepare_pull(
        (d_queries, own_grads[:, :head_dim].reshape(pair, 1, head_dim))
    )
    d_proj = jnp.concatenate(
        [
            d_query_pre.reshape(pair, group_width),
            d_key_pre.reshape(pair, head_dim),
            own_grads[:, head_dim:],
        ],
        axis=1,
    ).astype(BF)
    (d_proj,) = mark(d_proj)

    def rep_put(value, k):
        return Transfer(lax.ppermute(value, rep_axes, [(i, i ^ k) for i in range(reps)]))

    proj_parts = [
        jnp.concatenate([one, two], axis=1)
        for one, two in zip(
            head_order(columns(d_proj[:, :group_width])),
            reorder(columns(d_proj[:, group_width:]), rep_axes),
        )
    ]
    proj_sent = [rep_put(proj_parts[k], k) for k in range(1, reps)]
    down_grad.gather.next()
    (out_total,) = mark(out_scatter.total().astype(BF))
    waits(*proj_sent, *down_grad.gather.sent)
    proj_all = jnp.concatenate([proj_parts[0]] + [part.value for part in proj_sent], axis=0)
    (qkv_total,) = mark(dot_left_t(first_all, go(proj_all)[0]).astype(BF))

    def core_columns(value):
        return [jnp.where(core == c, value, jnp.zeros_like(value)) for c in range(cores)]

    (attention_terms,) = mark(
        jnp.concatenate(
            core_columns(qkv_total) + core_columns(out_total) + [laurel_terms], axis=1
        )
    )
    attention_sum = lax.psum_scatter(
        attention_terms, shard_axes, scatter_dimension=0, tiled=True
    )
    gate_grad.spread()
    (norm_sum,) = mark(dot_right_t(go(d_proj)[0], qkv_part))
    norm_sent = put(norm_sum[tokens:], "core")
    waits(norm_sent, *gate_grad.gather.sent)
    gate_grad.gather.next()
    d_first_norm = (
        norm_sum[:tokens]
        + norm_sent.value
        + dot_right_t(d_middle_low, down_low_full)
        + d_branch
    )
    d_input_part, grad_gain_zero = norm_one_pull(d_first_norm)
    grad_hidden, grad_gain_zero = mark(d_branch + d_input_part, grad_gain_zero)
    model_part = jnp.stack(
        [
            grad_gain_zero,
            grad_gain_one,
            grad_gain_two,
            grad_gain_three,
            grad_gain_four,
            grad_gain_five,
        ]
    )
    head_part = jnp.stack([grad_query_gain, grad_key_gain])
    gains = jnp.concatenate([model_part.reshape(-1, head_dim), head_part], axis=0)
    gain_axes = rep_axes + line_axes + ("core",)

    def gain_put(pair_axes):
        if len(pair_axes) == 1:
            return [put(gains, pair_axes[0])]
        across = lax.ppermute(gains, pair_axes, [(i, 3 - i) for i in range(4)])
        return [put(gains, pair_axes[0]), put(gains, pair_axes[1]), Transfer(across)]

    def gain_sum(transfers):
        values = [transfer.value for transfer in transfers]
        if len(values) == 1:
            return gains + values[0]
        return (gains + values[0]) + (values[1] + values[2])

    gain_steps = [gain_axes[i : i + 2] for i in range(0, len(gain_axes), 2)]
    gain_sent = gain_put(gain_steps[0])
    grad_down = jnp.zeros((weight_rows, ffn_units), F32)
    grad_down = down_grad.place(grad_down, down_grad.gather.blocks(), 0)
    waits(*gain_sent, *gate_grad.gather.sent)
    up_grad.spread()
    gains = gain_sum(gain_sent)
    for step in gain_steps[1:-2]:
        gain_sent = gain_put(step)
        waits(*gain_sent)
        gains = gain_sum(gain_sent)
    grad_gate_up = jnp.zeros((weight_rows, 2 * ffn_units), F32)
    grad_gate_up = gate_grad.place(grad_gate_up, gate_grad.gather.blocks(), 0)
    waits(*up_grad.gather.sent)
    up_grad.gather.next()
    if staged:
        grad_gate_up = up_grad.place(grad_gate_up, up_grad.gather.near_blocks(), 0, ffn_units)
    waits(*up_grad.gather.sent)
    if staged:
        far_block = [up_grad.gather.far_block()]
        grad_gate_up = up_grad.place(grad_gate_up, far_block, 3, ffn_units)
    else:
        grad_gate_up = up_grad.place(grad_gate_up, up_grad.gather.blocks(), 0, ffn_units)
    (attention_sum,) = go(attention_sum)
    attention_width = cores * (part + query_part)
    attention_gather = Gather(attention_sum[:, :attention_width], rep_axes, order)
    laurel_sum = attention_sum[:, attention_width:]
    laurel_sent = put(laurel_sum, rep_axes[0])
    gain_sent = gain_put(gain_steps[-2])
    waits(laurel_sent, *gain_sent, *attention_gather.sent)
    gains = gain_sum(gain_sent)
    gain_sent = gain_put(gain_steps[-1])
    attention_gather.next()
    for axis in rep_axes[1:]:
        laurel_sum = combine(laurel_sum, laurel_sent.value)
        laurel_sent = put(laurel_sum, axis)
    waits(laurel_sent, *gain_sent, *attention_gather.sent)
    gains = gain_sum(gain_sent)
    attention_blocks = reorder(attention_gather.blocks(), rep_axes)
    grad_qkv = jnp.concatenate(
        [
            block[:, c * part : c * part + query_part].astype(F32)
            for c in range(cores)
            for block in attention_blocks
        ]
        + [
            block[:, c * part + query_part : (c + 1) * part].astype(F32)
            for half in (attention_blocks[: reps // 2], attention_blocks[reps // 2 :])
            for c in range(cores)
            for block in half
        ],
        axis=1,
    )
    grad_out = jnp.concatenate(
        [
            block[:, cores * part + c * query_part : cores * part + (c + 1) * query_part].astype(
                F32
            )
            for c in range(cores)
            for block in attention_blocks
        ],
        axis=1,
    )
    laurel_sum = laurel_sum.astype(F32) + laurel_sent.value.astype(F32)
    grad_laurel_down, grad_laurel_up = laurel_sum[:, :rank], laurel_sum[:, rank:]
    grad_layer_gate, grad_layer_project = ple_sum[:, :ple], ple_sum[:, ple:]
    grad_model_gains = gains[: -head_part.shape[0]].reshape(model_part.shape)
    grad_head_gains = gains[-head_part.shape[0] :]
    return (
        layer_out,
        grad_hidden,
        grad_vectors,
        grad_model_gains,
        grad_head_gains,
        grad_qkv,
        grad_out,
        grad_laurel_down,
        grad_laurel_up,
        grad_gate_up,
        grad_down,
        grad_layer_gate,
        grad_layer_project,
    )


def solution(mesh):
    reps, shards = mesh.shape["rep"], mesh.shape["shard"]
    rep_axes = tuple(f"rep{i}" for i in range(reps.bit_length() - 1))
    line_axes = tuple(f"line{i}" for i in range(shards.bit_length() - 2))
    axes = rep_axes + line_axes + ("core",)
    assert 1 << len(axes) == reps * shards
    fine = Mesh(np.asarray(mesh.devices).reshape((2,) * len(axes)), axes)
    rows, owned = P(axes, None), P(line_axes + ("core",), None)
    return jax.shard_map(
        functools.partial(body, rep_axes, line_axes),
        mesh=fine,
        in_specs=(rows, rows, P(axes), rows, P(), P()) + (owned,) * 8,
        out_specs=(rows, rows, rows, P(), P()) + (owned,) * 8,
        check_vma=False,
    )
```
